128 devices in a mesh: ctx: 8 (over x, core), ch: 16 (over y, z).
Axes of the slice: x: 4, y: 4, z: 4, core: 2. Of those that a mesh axis runs over, the one named last changes fastest.
Arguments:
- inputs: bfloat16 [2, 1024, 8192], P(None, 'ctx', 'ch'), may hold values from -6 to 6
- gates: bfloat16 [2, 1024, 8192], P(None, 'ctx', 'ch'), may hold values from -6 to 6
- conv_weight: float32 [4, 8192], P(None, 'ch'), may hold values from -3 to 3
- conv_bias: float32 [8192], P('ch'), may hold values from -3 to 3
- x_weight: bfloat16 [8192, 288], P('ch'), may hold values from -0.0625 to 0.0625
- dt_weight: bfloat16 [256, 8192], P(None, 'ch'), may hold values from -0.9375 to 0.9375
- dt_bias: float32 [8192], P('ch'), may hold values from -5 to -2
- decay_rate: float32 [16, 8192], P(None, 'ch'), may hold values from 9.765625e-06 to 1
- skip: float32 [8192], P('ch'), may hold values from 0.5 to 1.5
- lengths: int32 [2], replicated, may hold values from 256 to 1024, as said below
- row_request: int32 [512], P('ctx'), may hold values from 0 to 1
- dec_inputs: bfloat16 [4, 512, 8192], P(None, 'ctx', 'ch'), may hold values from -6 to 6
- dec_gates: bfloat16 [4, 512, 8192], P(None, 'ctx', 'ch'), may hold values from -6 to 6
Outputs:
- prefill_out: bfloat16 [2, 1024, 8192], P(None, 'ctx', 'ch')
- decode_out: bfloat16 [4, 512, 8192], P(None, 'ctx', 'ch')
The draws below stay inside these ranges and needn't reach their ends.
Inputs may be any that keep to these rules, and one draw needn't show every extreme that they name: `lengths`: every length is at least 256, and some request has length 1024.
All inputs are finite; a program needn't handle non-finite values.
Results may differ from the reference program's by a relative error of at most 0.015.
Values may be sent and summed in bfloat16 or wider, within the bound.
A program may use at most 128 MiB of HBM per device.

```python
import math
import jax
import jax.numpy as jnp
from jax import lax

E = 8192
N = 16
R = 256
KCONV = 4
BLK = 128
STEPS = 4
REQS = 2
SEQ = 1024
ROWS = 512


def draw_lengths(key, part):
    key = jax.random.fold_in(key, 7)
    first, second = jax.random.split(key)
    values = jax.random.randint(first, (REQS,), SEQ // 4, SEQ + 1)
    longest = jax.random.randint(second, (), 0, REQS)
    return jnp.where(jnp.arange(REQS) == longest, SEQ, values).astype(jnp.int32)


def plant(entries, rng, low, top_value):
    longest = entries.shape.index(max(entries.shape))
    spots = []
    for shift in (0, 1):
        where = [jax.random.randint(jax.random.fold_in(rng, axis), (), 0, length) for axis, length in enumerate(entries.shape)]
        where[longest] = (where[longest] + shift) % entries.shape[longest]
        spots.append(tuple(where))
    return entries.at[spots[0]].set(low).at[spots[1]].set(top_value)


def steps_of(rng, dims, shards, low, high):
    level, own = 1.0, jax.random.fold_in(rng, 6)
    for axis_at, blocks in shards:
        steps = jnp.exp(jax.random.uniform(jax.random.fold_in(own, axis_at), (blocks,), jnp.float32, low / len(shards), high / len(shards)))
        level = level * jnp.repeat(steps, dims[axis_at] // blocks).reshape([-1 if axis == axis_at else 1 for axis in range(len(dims))])
    return level


def gaussian(own_key, dims, deviation, limit, shards=(), kind=jnp.bfloat16):
    array = jax.random.normal(own_key, dims, jnp.float32) * deviation
    if len(shards) > 0:
        array = steps_of(own_key, dims, shards, -0.22, 0.18) * array
    return jnp.clip(array, min=-limit, max=limit).astype(kind)


def setup_inputs(seed: int = 0) -> dict:
    keys = jax.random.split(jax.random.key(seed), 14)
    return {
        "inputs": gaussian(keys[0], (REQS, SEQ, E), 1.0, 6.0, ((1, 8), (2, 16))),
        "gates": gaussian(keys[1], (REQS, SEQ, E), 1.0, 6.0, ((1, 8), (2, 16))),
        "conv_weight": gaussian(keys[2], (KCONV, E), 0.5, 3.0, ((1, 16),), jnp.float32),
        "conv_bias": gaussian(keys[3], (E,), 0.5, 3.0, ((0, 16),), jnp.float32),
        "x_weight": gaussian(keys[4], (E, R + 2 * N), E ** -0.5, 0.0625, ((0, 16),)),
        "dt_weight": gaussian(keys[5], (R, E), (3.0 * R ** -0.5), 0.9375, ((1, 16),)),
        "dt_bias": jnp.clip(-5.0 + 3.0 * jax.random.uniform(keys[6], (E,), jnp.float32) ** steps_of(keys[6], (E,), ((0, 16),), -0.2, 0.2), -5.0, -2.0),
        "decay_rate": jnp.clip(jnp.exp(math.log(1.0) - 11.536642 * jax.random.uniform(keys[7], (N, E), jnp.float32) ** steps_of(keys[7], (N, E), ((1, 16),), -0.2, 0.2)), 9.765624781721272e-06, 1.0),
        "skip": jnp.clip(0.5 + 1.0 * jax.random.uniform(keys[8], (E,), jnp.float32) ** steps_of(keys[8], (E,), ((0, 16),), -0.2, 0.2), 0.5, 1.5),
        "lengths": draw_lengths(jax.random.fold_in(keys[13], 71), 0),
        "row_request": plant(jax.random.randint(keys[10], (ROWS,), 0, REQS), jax.random.fold_in(keys[10], 1), 0, REQS - 1).astype(jnp.int32),
        "dec_inputs": gaussian(keys[11], (STEPS, ROWS, E), 1.0, 6.0, ((1, 8), (2, 16))),
        "dec_gates": gaussian(keys[12], (STEPS, ROWS, E), 1.0, 6.0, ((1, 8), (2, 16))),
    }


def combine(earlier, later):
    return earlier[0] * later[0], later[0] * earlier[1] + later[1]


def project(u, x_weight, dt_weight, dt_bias, rank):
    flat = u.reshape(-1, u.shape[-1])
    proj = jnp.dot(flat, x_weight, preferred_element_type=jnp.float32)
    step = jnp.dot(proj[:, :rank].astype(jnp.bfloat16), dt_weight, preferred_element_type=jnp.float32)
    step = jax.nn.softplus(step + dt_bias)
    return proj, step


def reference(inputs, gates, conv_weight, conv_bias, x_weight, dt_weight, dt_bias, decay_rate, skip, lengths, row_request, dec_inputs, dec_gates):
    nblk = SEQ // BLK
    xs = jnp.moveaxis(inputs.reshape(REQS, nblk, BLK, E), 1, 0)
    zs = jnp.moveaxis(gates.reshape(REQS, nblk, BLK, E), 1, 0)

    def block(carry, item):
        state, tail, final, start = carry
        xblk, zblk = item
        ext = jnp.concatenate([tail, xblk.astype(jnp.float32)], axis=1)
        conv = conv_bias + sum(conv_weight[k] * ext[:, k:k + BLK] for k in range(KCONV))
        u = jax.nn.silu(conv).astype(jnp.bfloat16)
        proj, step = project(u, x_weight, dt_weight, dt_bias, R)
        proj = proj.reshape(REQS, BLK, -1)
        step = step.reshape(REQS, BLK, E)
        bin_ = proj[..., R:R + N]
        cout = proj[..., R + N:]
        uf = u.astype(jnp.float32)
        decay = jnp.exp(-step[:, :, None, :] * decay_rate)
        drive = (step * uf)[:, :, None, :] * bin_[:, :, :, None]
        acum, bcum = lax.associative_scan(combine, (decay, drive), axis=1)
        hs = acum * state[:, None] + bcum
        pos = start + jnp.arange(BLK, dtype=jnp.int32)
        live = (pos[None, :] < lengths[:, None]).astype(jnp.float32)
        out = (jnp.einsum('rtn,rtne->rte', cout, hs) + skip * uf) * jax.nn.silu(zblk.astype(jnp.float32))
        out = (out * live[:, :, None]).astype(jnp.bfloat16)
        pick = (pos[None, :] == lengths[:, None] - 1).astype(jnp.float32)
        final = final + jnp.einsum('rt,rtne->rne', pick, hs)
        return (hs[:, -1], ext[:, BLK:], final, start + BLK), out

    init = (jnp.zeros((REQS, N, E), jnp.float32), jnp.zeros((REQS, KCONV - 1, E), jnp.float32),
            jnp.zeros((REQS, N, E), jnp.float32), jnp.int32(0))
    carry, outs = lax.scan(block, init, (xs, zs))
    final = carry[2]
    prefill_out = jnp.moveaxis(outs, 0, 1).reshape(REQS, SEQ, E)

    def window_of(row, length):
        return lax.dynamic_slice(row, ((length - KCONV + 1).astype(jnp.int32), jnp.int32(0)), (KCONV - 1, E))

    window = jax.vmap(window_of)(inputs, lengths).astype(jnp.float32)
    hidden = final[row_request]
    recent = window[row_request]
    results = []
    for step_no in range(STEPS):
        xnew = dec_inputs[step_no].astype(jnp.float32)
        ext = jnp.concatenate([recent, xnew[:, None]], axis=1)
        conv = conv_bias + sum(conv_weight[k] * ext[:, k] for k in range(KCONV))
        u = jax.nn.silu(conv).astype(jnp.bfloat16)
        proj, step = project(u, x_weight, dt_weight, dt_bias, R)
        uf = u.astype(jnp.float32)
        hidden = jnp.exp(-step[:, None, :] * decay_rate) * hidden + (step * uf)[:, None, :] * proj[:, R:R + N, None]
        out = (jnp.einsum('in,ine->ie', proj[:, R + N:], hidden) + skip * uf) * jax.nn.silu(dec_gates[step_no].astype(jnp.float32))
        results.append(out.astype(jnp.bfloat16))
        recent = ext[:, 1:]
    return prefill_out, jnp.stack(results)
```

```python
import functools
import math

import jax
import jax.numpy as jnp
from jax import lax
from jax.experimental import pallas as pl
from jax.experimental.pallas import tpu as pltpu
from jax.sharding import PartitionSpec as P

MESH = pl.DeviceIdType.MESH
F32 = jnp.float32
BF16 = jnp.bfloat16
LOG2E = math.log2(math.e)
KCONV = 4
SEG = 8
LANES = 128


def softplus(x):
    return jnp.maximum(x, 0.0) + jnp.log1p(jnp.exp(-jnp.abs(x)))


def silu(x):
    return x / (1.0 + jnp.exp(-x))


def row_of(value, rows=SEG):
    return jnp.broadcast_to(value, (rows, value.shape[1]))


def kernel(
    nctx, nch,
    x_ref, gate_ref, cw_ref, cb_ref, xw_ref, dtw_ref, dtb_ref, a_ref, skip_ref, len_ref, req_ref, dx_ref, dg_ref,
    out_ref, dout_ref,
    hw, xe, u_pre, u_dec, send_pre, send_dec, rs_pre, rs_dec, ag_pre, ag_dec, wx, a2, dt_pre, dt_dec, bc_pre, bc_dec,
    d_all, e_all, ssum, st32, states, hexcl, sexcl, prefix, y_pre, y_dec, mask_dec,
    hw_send, hw_recv, rsp_send, rsp_recv, rsd_send, rsd_recv, agp_send, agp_recv, agd_send, agd_recv,
    ss_send, ss_recv, st_send, st_recv,
):
    nreq, seq, width = x_ref.shape
    steps, drows = dx_ref.shape[0], dx_ref.shape[1]
    nstate = a_ref.shape[0]
    rank = dtw_ref.shape[0]
    tokens = nreq * seq
    dtokens = steps * drows
    nj = seq // SEG
    chunks = width // LANES
    nrc = nreq * chunks
    part = tokens // nch
    cols = rank + LANES
    me_ctx = lax.axis_index("ctx")
    me_ch = lax.axis_index("ch")
    offset = me_ctx * seq

    def peer(axis, me, count, k):
        return {axis: lax.rem(me + k, count)}

    barrier = pltpu.get_barrier_semaphore()
    for k in range(1, nctx):
        pl.semaphore_signal(barrier, inc=1, device_id=peer("ctx", me_ctx, nctx, k), device_id_type=MESH)
    for k in range(1, nch):
        pl.semaphore_signal(barrier, inc=1, device_id=peer("ch", me_ch, nch, k), device_id_type=MESH)

    def spread(axis, me, count, src, dst, send_sem, recv_sem):
        for k in range(1, count):
            pltpu.make_async_remote_copy(
                src_ref=src(k), dst_ref=dst(k), send_sem=send_sem, recv_sem=recv_sem,
                device_id=peer(axis, me, count, k), device_id_type=MESH,
            ).start()

    def all_of(ref, count, sem):
        view = ref.at[pl.ds(0, count - 1)]
        pltpu.make_async_copy(view, view, sem).wait()

    x2 = x_ref[...].reshape(tokens, width)
    q = lax.broadcasted_iota(jnp.int32, (16, tokens), 0)
    col = lax.broadcasted_iota(jnp.int32, (16, tokens), 1)
    win = q >= 6
    q6 = jnp.where(win, q - 6, q)
    second = q6 >= 3
    tap = jnp.where(second, q6 - 3, q6)
    length = jnp.where(second, len_ref[1], len_ref[0])
    target = jnp.where(win, length - (KCONV - 1) + tap - offset, seq - (KCONV - 1) + tap)
    good = (target >= 0) & (target < seq) & (q < 12)
    place = jnp.where(second, seq, 0) + target
    pick = jnp.where(good & (col == place), 1.0, 0.0).astype(BF16)
    hw[me_ctx] = jnp.dot(pick, x2, preferred_element_type=F32).astype(BF16)

    pl.semaphore_wait(barrier, nctx + nch - 2)
    spread("ctx", me_ctx, nctx, lambda k: hw.at[me_ctx], lambda k: hw.at[me_ctx], hw_send, hw_recv)

    i0 = lax.broadcasted_iota(jnp.int32, (seq, seq), 0)
    i1 = lax.broadcasted_iota(jnp.int32, (seq, seq), 1)
    perm = jnp.where(i1 == (i0 % SEG) * nj + i0 // SEG, 1.0, 0.0).astype(BF16)
    for r in range(nreq):
        xe[r, pl.ds(3 * SEG, seq), :] = jnp.dot(perm, x_ref[r], preferred_element_type=F32)
    k0 = lax.broadcasted_iota(jnp.int32, (2 * nstate, LANES), 0)
    k1 = lax.broadcasted_iota(jnp.int32, (2 * nstate, LANES), 1)
    twice = jnp.where((k1 == k0) | (k1 == k0 + 2 * nstate), 1.0, 0.0).astype(BF16)
    wx[:, pl.ds(0, rank)] = xw_ref[:, pl.ds(0, rank)]
    wx[:, pl.ds(rank, LANES)] = jnp.dot(
        xw_ref[:, pl.ds(rank, 2 * nstate)], twice, preferred_element_type=F32
    ).astype(BF16)
    a2[...] = a_ref[...] * (-LOG2E)
    req = jnp.broadcast_to(req_ref[...].reshape(1, drows), (drows, drows))
    d0 = lax.broadcasted_iota(jnp.int32, (drows, drows), 0)
    d1 = lax.broadcasted_iota(jnp.int32, (drows, drows), 1)
    request = jnp.sum(jnp.where((d0 == d1) & (req == 1), 1.0, 0.0), axis=1, keepdims=True)
    mask_dec[...] = jnp.broadcast_to(request, (drows, LANES))
    cb = cb_ref[...].reshape(1, width)
    dtb = dtb_ref[...].reshape(1, width)
    skip = skip_ref[...].reshape(1, width)

    lane = lax.broadcasted_iota(jnp.int32, (1, LANES), 1)
    low = lane < 2 * nstate
    high = (lane >= 2 * nstate) & (lane < 4 * nstate)

    def split(value):
        top = value.astype(BF16).astype(F32)
        return jnp.where(low, top, jnp.where(high, value - top, 0.0)).astype(BF16)

    def project(u, send):
        proj = jnp.dot(u, wx[...], preferred_element_type=F32)
        send[:, :, pl.ds(0, rank)] = proj[:, :rank].astype(BF16).reshape(nch, part, rank)
        send[:, :, pl.ds(rank, LANES)] = split(proj[:, rank:]).reshape(nch, part, LANES)

    all_of(hw, nctx, hw_recv)
    before = hw[lax.rem(me_ctx + nctx - 1, nctx)].astype(F32)
    before = jnp.where(me_ctx > 0, before, 0.0)
    sub = lax.broadcasted_iota(jnp.int32, (SEG, width), 0)
    for r in range(nreq):
        for k in range(KCONV - 1):
            last = xe[r, pl.ds((nj + k) * SEG, SEG), :]
            entry = row_of(before[3 * r + k : 3 * r + k + 1])
            xe[r, pl.ds(k * SEG, SEG), :] = jnp.where(sub == 0, entry, pltpu.roll(last, 1, 0))
        conv = cb + sum(cw_ref[k : k + 1] * xe[r, pl.ds(k * SEG, seq), :] for k in range(KCONV))
        u_pre[pl.ds(r * seq, seq), :] = silu(conv).astype(BF16).astype(F32)
    project(u_pre[...].astype(BF16), send_pre)
    spread(
        "ch", me_ch, nch, lambda k: send_pre.at[lax.rem(me_ch + k, nch)], lambda k: rs_pre.at[k - 1], rsp_send, rsp_recv
    )

    window = hw[0].astype(F32)
    for i in range(1, nctx):
        window = window + hw[i].astype(F32)
    chosen = jnp.broadcast_to(request, (drows, width)) > 0.5
    recent = [
        jnp.where(chosen, row_of(window[9 + k : 10 + k], drows), row_of(window[6 + k : 7 + k], drows))
        for k in range(KCONV - 1)
    ]
    recent = recent + [dx_ref[s].astype(F32) for s in range(steps)]
    for s in range(steps):
        conv = cb + sum(cw_ref[k : k + 1] * recent[s + k] for k in range(KCONV))
        u_dec[pl.ds(s * drows, drows), :] = silu(conv).astype(BF16).astype(F32)
    project(u_dec[...].astype(BF16), send_dec)
    spread(
        "ch", me_ch, nch, lambda k: send_dec.at[lax.rem(me_ch + k, nch)], lambda k: rs_dec.at[k - 1], rsd_send, rsd_recv
    )

    def reduce(send, rs, ag, rs_recv, ag_send, ag_recv):
        all_of(rs, nch, rs_recv)
        total = send[me_ch].astype(F32)
        for k in range(nch - 1):
            total = total + rs[k].astype(F32)
        tail = total[:, rank:]
        tail = tail + pltpu.roll(tail, 2 * nstate, 1) + pltpu.roll(tail, LANES - 2 * nstate, 1)
        ag[me_ch, :, pl.ds(0, rank)] = total[:, :rank].astype(BF16)
        ag[me_ch, :, pl.ds(rank, LANES)] = split(tail)
        spread("ch", me_ch, nch, lambda k: ag.at[me_ch], lambda k: ag.at[me_ch], ag_send, ag_recv)

    reduce(send_pre, rs_pre, ag_pre, rsp_recv, agp_send, agp_recv)
    reduce(send_dec, rs_dec, ag_dec, rsd_recv, agd_send, agd_recv)

    def expand(ag, bc):
        w0 = lax.broadcasted_iota(jnp.int32, (LANES, 2 * nstate * LANES), 0)
        w1 = lax.broadcasted_iota(jnp.int32, (LANES, 2 * nstate * LANES), 1) // LANES
        copies = jnp.where((w0 == w1) | (w0 == w1 + 2 * nstate), 1.0, 0.0).astype(BF16)
        maps = ag[:, :, pl.ds(rank, LANES)].reshape(nch * part, LANES)
        bc[...] = jnp.dot(maps, copies, preferred_element_type=F32)

    def step_sizes(ag):
        ranks = ag[:, :, pl.ds(0, rank)].reshape(nch * part, rank)
        return softplus(jnp.dot(ranks, dtw_ref[...], preferred_element_type=F32) + dtb)

    all_of(ag_pre, nch, agp_recv)
    row = lax.broadcasted_iota(jnp.int32, (seq, 1), 0)
    token = offset + (row % SEG) * nj + row // SEG
    sizes = step_sizes(ag_pre)
    for r in range(nreq):
        own = jnp.where(token < len_ref[r], sizes[r * seq : (r + 1) * seq], 0.0)
        dt_pre[pl.ds(r * seq, seq), :] = own
        whole = jnp.sum(own, axis=0, keepdims=True)
        for c in range(chunks):
            ssum[me_ctx, pl.ds(r * chunks + c, 1), :] = whole[:, c * LANES : (c + 1) * LANES]
    spread("ctx", me_ctx, nctx, lambda k: ssum.at[me_ctx], lambda k: ssum.at[me_ctx], ss_send, ss_recv)
    expand(ag_pre, bc_pre)

    sub1 = lax.broadcasted_iota(jnp.int32, (SEG, LANES), 0)

    def lanes_of(c):
        return pl.ds(pl.multiple_of(c * LANES, LANES), LANES)

    def rates(lanes):
        return [row_of(a2[n : n + 1, lanes]) for n in range(nstate)]

    def first_pass(rc, carry):
        r, c = rc // chunks, rc % chunks
        lanes = lanes_of(c)
        rate = rates(lanes)
        h = [None] * nstate
        total = None
        for j in range(nj):
            rows = pl.ds(pl.multiple_of(r * seq + j * SEG, SEG), SEG)
            dt = dt_pre[rows, lanes]
            dtu = dt * u_pre[rows, lanes]
            total = dt if j == 0 else total + dt
            for n in range(nstate):
                decay = jnp.exp2(dt * rate[n])
                d_all[rc, j, n] = decay
                drive = dtu * bc_pre[rows, n * LANES : (n + 1) * LANES]
                h[n] = drive if j == 0 else decay * h[n] + drive
        for k in (1, 2, 4):
            for n in range(nstate):
                h[n] = h[n] + jnp.exp2(rate[n] * total) * jnp.where(sub1 >= k, pltpu.roll(h[n], k, 0), 0.0)
            total = total + jnp.where(sub1 >= k, pltpu.roll(total, k, 0), 0.0)
        sexcl[rc] = jnp.where(sub1 >= 1, pltpu.roll(total, 1, 0), 0.0)
        for n in range(nstate):
            st32[rc, n : n + 1, :] = h[n][SEG - 1 :]
            hexcl[rc, n] = jnp.where(sub1 >= 1, pltpu.roll(h[n], 1, 0), 0.0)
        states[me_ctx, rc] = st32[rc].astype(BF16)
        return carry

    lax.fori_loop(0, nrc, first_pass, 0)
    spread("ctx", me_ctx, nctx, lambda k: states.at[me_ctx], lambda k: states.at[me_ctx], st_send, st_recv)

    all_of(ag_dec, nch, agd_recv)
    dt_dec[...] = step_sizes(ag_dec)
    expand(ag_dec, bc_dec)
    groups = drows // SEG

    for c in range(chunks):
        prefix[nrc, 0, c : c + 1, :] = skip[:, c * LANES : (c + 1) * LANES]

    def skip_at(c):
        return row_of(prefix[nrc, 0, pl.ds(c, 1), :])

    def decode_local(gc, carry):
        g, c = gc // chunks, gc % chunks
        lanes = lanes_of(c)
        rate = rates(lanes)
        h, product = [None] * nstate, [None] * nstate
        for s in range(steps):
            rows = pl.ds(pl.multiple_of(s * drows + g * SEG, SEG), SEG)
            dt = dt_dec[rows, lanes]
            u = u_dec[rows, lanes]
            dtu = dt * u
            y = skip_at(c) * u
            for n in range(nstate):
                decay = jnp.exp2(dt * rate[n])
                cout = bc_dec[rows, (nstate + n) * LANES : (nstate + n + 1) * LANES]
                drive = dtu * bc_dec[rows, n * LANES : (n + 1) * LANES]
                h[n] = drive if s == 0 else decay * h[n] + drive
                product[n] = decay if s == 0 else decay * product[n]
                y = y + cout * h[n]
                e_all[gc, s, n] = cout * product[n]
            y_dec[rows, lanes] = y
        return carry

    lax.fori_loop(0, groups * chunks, decode_local, 0)

    all_of(ssum, nctx, ss_recv)
    all_of(states, nctx, st_recv)

    def combine(rc, carry):
        c = rc % chunks
        rate = a2[:, lanes_of(c)]
        h = jnp.zeros((nstate, LANES), F32)
        for i in range(nctx):
            prefix[rc, i] = h
            h = jnp.exp2(rate * row_of(ssum[i, pl.ds(rc, 1), :], nstate)) * h + states[i, rc].astype(F32)
        prefix[rc, nctx] = h
        return carry

    lax.fori_loop(0, nrc, combine, 0)

    def second_pass(rc, carry):
        r, c = rc // chunks, rc % chunks
        lanes = lanes_of(c)
        rate = rates(lanes)
        start = sexcl[rc]
        h = [
            hexcl[rc, n] + jnp.exp2(rate[n] * start) * row_of(prefix[rc, me_ctx, n : n + 1, :])
            for n in range(nstate)
        ]
        for j in range(nj):
            rows = pl.ds(pl.multiple_of(r * seq + j * SEG, SEG), SEG)
            u = u_pre[rows, lanes]
            dtu = dt_pre[rows, lanes] * u
            y = skip_at(c) * u
            for n in range(nstate):
                h[n] = d_all[rc, j, n] * h[n] + dtu * bc_pre[rows, n * LANES : (n + 1) * LANES]
                y = y + bc_pre[rows, (nstate + n) * LANES : (nstate + n + 1) * LANES] * h[n]
            y_pre[rc, pl.ds(j, SEG, stride=nj), :] = y
        return carry

    lax.fori_loop(0, nrc, second_pass, 0)

    def decode_rest(gc, carry):
        g, c = gc // chunks, gc % chunks
        lanes = lanes_of(c)
        mine = mask_dec[pl.ds(pl.multiple_of(g * SEG, SEG), SEG), :] > 0.5
        h = [
            jnp.where(
                mine,
                row_of(prefix[chunks + c, nctx, n : n + 1, :]),
                row_of(prefix[c, nctx, n : n + 1, :]),
            )
            for n in range(nstate)
        ]
        for s in range(steps):
            rows = pl.ds(pl.multiple_of(s * drows + g * SEG, SEG), SEG)
            y = y_dec[rows, lanes]
            for n in range(nstate):
                y = y + e_all[gc, s, n] * h[n]
            y_dec[rows, lanes] = y
        return carry

    lax.fori_loop(0, groups * chunks, decode_rest, 0)

    natural = offset + lax.broadcasted_iota(jnp.int32, (seq, 1), 0)
    for r in range(nreq):
        live = natural < len_ref[r]
        for c in range(chunks):
            lanes = pl.ds(c * LANES, LANES)
            y = y_pre[r * chunks + c] * silu(gate_ref[r, :, lanes].astype(F32))
            out_ref[r, :, lanes] = jnp.where(live, y, 0.0).astype(BF16)
    for s in range(steps):
        dout_ref[s] = (y_dec[pl.ds(s * drows, drows), :] * silu(dg_ref[s].astype(F32))).astype(BF16)

    all_of(hw, nctx, hw_send)
    all_of(rs_pre, nch, rsp_send)
    all_of(rs_dec, nch, rsd_send)
    all_of(ag_pre, nch, agp_send)
    all_of(ag_dec, nch, agd_send)
    all_of(ssum, nctx, ss_send)
    all_of(states, nctx, st_send)


def on_device(nctx, nch, *args):
    inputs, dt_weight, decay_rate, dec_inputs = args[0], args[5], args[7], args[11]
    nreq, seq, width = inputs.shape
    steps, drows = dec_inputs.shape[:2]
    rank, nstate = dt_weight.shape[0], decay_rate.shape[0]
    tokens, dtokens = nreq * seq, steps * drows
    nj, chunks, groups = seq // SEG, width // LANES, drows // SEG
    nrc = nreq * chunks
    cols = rank + LANES
    vmem = pl.BlockSpec(memory_space=pltpu.VMEM)
    smem = pl.BlockSpec(memory_space=pltpu.SMEM)
    sem = pltpu.SemaphoreType.DMA
    scratch = [
        pltpu.VMEM((nctx, 16, width), BF16),
        pltpu.VMEM((nreq, (nj + KCONV - 1) * SEG, width), F32),
        pltpu.VMEM((tokens, width), F32),
        pltpu.VMEM((dtokens, width), F32),
        pltpu.VMEM((nch, tokens // nch, cols), BF16),
        pltpu.VMEM((nch, dtokens // nch, cols), BF16),
        pltpu.VMEM((nch - 1, tokens // nch, cols), BF16),
        pltpu.VMEM((nch - 1, dtokens // nch, cols), BF16),
        pltpu.VMEM((nch, tokens // nch, cols), BF16),
        pltpu.VMEM((nch, dtokens // nch, cols), BF16),
        pltpu.VMEM((width, cols), BF16),
        pltpu.VMEM((nstate, width), F32),
        pltpu.VMEM((tokens, width), F32),
        pltpu.VMEM((dtokens, width), F32),
        pltpu.VMEM((tokens, 2 * nstate * LANES), F32),
        pltpu.VMEM((dtokens, 2 * nstate * LANES), F32),
        pltpu.VMEM((nrc, nj, nstate, SEG, LANES), F32),
        pltpu.VMEM((groups * chunks, steps, nstate, SEG, LANES), F32),
        pltpu.VMEM((nctx, nrc, LANES), F32),
        pltpu.VMEM((nrc, nstate, LANES), F32),
        pltpu.VMEM((nctx, nrc, nstate, LANES), BF16),
        pltpu.VMEM((nrc, nstate, SEG, LANES), F32),
        pltpu.VMEM((nrc, SEG, LANES), F32),
        pltpu.VMEM((nrc + 1, nctx + 1, nstate, LANES), F32),
        pltpu.VMEM((nrc, seq, LANES), F32),
        pltpu.VMEM((dtokens, width), F32),
        pltpu.VMEM((drows, LANES), F32),
    ] + [sem] * 14
    return pl.pallas_call(
        functools.partial(kernel, nctx, nch),
        out_shape=(
            jax.ShapeDtypeStruct(inputs.shape, BF16),
            jax.ShapeDtypeStruct(dec_inputs.shape, BF16),
        ),
        in_specs=[vmem] * 9 + [smem] + [vmem] * 3,
        out_specs=(vmem, vmem),
        scratch_shapes=scratch,
        compiler_params=pltpu.CompilerParams(
            collective_id=0, has_side_effects=True, vmem_limit_bytes=56 * 1024 * 1024
        ),
    )(*args)


def solution(mesh):
    placed = (
        P(None, "ctx", "ch"),
        P(None, "ctx", "ch"),
        P(None, "ch"),
        P("ch"),
        P("ch", None),
        P(None, "ch"),
        P("ch"),
        P(None, "ch"),
        P("ch"),
        P(),
        P("ctx"),
        P(None, "ctx", "ch"),
        P(None, "ctx", "ch"),
    )
    return jax.shard_map(
        functools.partial(on_device, mesh.shape["ctx"], mesh.shape["ch"]),
        mesh=mesh,
        in_specs=placed,
        out_specs=(P(None, "ctx", "ch"), P(None, "ctx", "ch")),
        check_vma=False,
    )
```

```python
import functools
import math

import jax
import jax.numpy as jnp
from jax import lax
from jax.experimental import pallas as pl
from jax.experimental.pallas import tpu as pltpu
from jax.sharding import PartitionSpec as P

MESH = pl.DeviceIdType.MESH
F32 = jnp.float32
BF16 = jnp.bfloat16
LOG2E = math.log2(math.e)
KCONV = 4
SEG = 8
LANES = 128
SIDE = 4


def softplus(x):
    return jnp.maximum(x, 0.0) + jnp.log1p(jnp.exp(-jnp.abs(x)))


def silu(x):
    return x / (1.0 + jnp.exp(-x))


def row_of(value, rows=SEG):
    return jnp.broadcast_to(value, (rows, value.shape[1]))


def total_of(terms):
    while len(terms) > 1:
        terms = [a + b for a, b in zip(terms[::2], terms[1::2])] + ([terms[-1]] if len(terms) % 2 else [])
    return terms[0]


def ring(d):
    return min(d, SIDE - d)


def kernel(
    nctx, nch,
    x_hbm, gate_hbm, cw_hbm, cb_hbm, xw_hbm, dtw_hbm, dtb_hbm, a_hbm, skip_hbm, len_ref, req_hbm, dx_hbm, dg_hbm,
    out_ref, dout_ref,
    x_ref, gate_ref, cw_ref, cb_ref, xw_ref, dtw_ref, dtb_ref, a_ref, skip_ref, req_ref, dx_ref, dg_ref,
    hw, xe, u_pre, u_dec, edge_u, edge, send_pre, send_dec, rs_pre, rs_dec, ag_pre, ag_dec, wx, a2, skips,
    dt_pre, dt_dec, bc_pre, bc_dec, d_all, e_pre, e_dec, ssum, st32, states, hexcl, sexcl, pseg, weight, prefix,
    y_loc, y_nat, y_dec, y_half, y_fin, g_pre, g_dec, mask_dec,
    in_sems, hw_send, hw_recv, ed_send, ed_recv, rsp_send, rsp_recv, rsd_send, rsd_recv,
    agp_send, agp_recv, agd_send, agd_recv, ss_send, ss_recv, st_send, st_recv,
):
    nreq, seq, width = x_ref.shape
    steps, drows = dx_ref.shape[0], dx_ref.shape[1]
    nstate = a_ref.shape[0]
    rank = dtw_ref.shape[0]
    tokens = nreq * seq
    nj = seq // SEG
    chunks = width // LANES
    nrc = nreq * chunks
    groups = drows // SEG
    part = tokens // nch
    me_ctx = lax.axis_index("ctx")
    me_ch = lax.axis_index("ch")
    offset = me_ctx * seq

    pairs = [
        (x_hbm, x_ref), (xw_hbm, xw_ref), (cw_hbm, cw_ref), (cb_hbm, cb_ref), (dx_hbm, dx_ref), (req_hbm, req_ref),
        (dtw_hbm, dtw_ref), (dtb_hbm, dtb_ref), (a_hbm, a_ref), (skip_hbm, skip_ref), (gate_hbm, gate_ref),
        (dg_hbm, dg_ref),
    ]
    loads = []
    for i, (src, dst) in enumerate(pairs):
        if dst.dtype == BF16 and len(dst.shape) == 3:
            pieces = [(k, pl.ds(j * 32, 32)) for k in range(dst.shape[0]) for j in range(dst.shape[1] // 32)]
        elif dst.dtype == BF16:
            pieces = [(pl.ds(j * 32, 32),) for j in range(dst.shape[0] // 32)]
        else:
            pieces = [None]
        sem = in_sems.at[i]
        for piece in pieces:
            if piece is None:
                pltpu.make_async_copy(src, dst, sem).start()
            else:
                pltpu.make_async_copy(src.at[piece], dst.at[piece], sem).start()
        loads.append(pltpu.make_async_copy(src, dst, sem))

    def far_ch():
        for k in sorted(range(1, nch), key=lambda k: -(ring(k // SIDE) + ring(k % SIDE))):
            y = lax.rem(me_ch // SIDE + k // SIDE, nch // SIDE)
            z = lax.rem(lax.rem(me_ch, SIDE) + k % SIDE, SIDE)
            yield k, y * SIDE + z

    def far_ctx():
        for k in sorted(range(1, nctx), key=lambda k: -ring(k // 2)):
            x = lax.rem(me_ctx // 2 + k // 2, nctx // 2)
            core = lax.rem(lax.rem(me_ctx, 2) + k % 2, 2)
            yield k, x * 2 + core

    far = {"ch": far_ch, "ctx": far_ctx}

    barrier = pltpu.get_barrier_semaphore()
    for axis in ("ch", "ctx"):
        for k, to in far[axis]():
            pl.semaphore_signal(barrier, inc=1, device_id={axis: to}, device_id_type=MESH)

    def spread(axis, src, dst, send_sem, recv_sem):
        for k, to in far[axis]():
            pltpu.make_async_remote_copy(
                src_ref=src(to), dst_ref=dst(k), send_sem=send_sem, recv_sem=recv_sem,
                device_id={axis: to}, device_id_type=MESH,
            ).start()

    def all_of(ref, count, sem):
        view = ref.at[pl.ds(0, count - 1)]
        pltpu.make_async_copy(view, view, sem).wait()

    i0 = lax.broadcasted_iota(jnp.int32, (seq, seq), 0)
    i1 = lax.broadcasted_iota(jnp.int32, (seq, seq), 1)
    perm = jnp.where(i1 == (i0 % SEG) * nj + i0 // SEG, 1.0, 0.0).astype(BF16)
    lane = lax.broadcasted_iota(jnp.int32, (1, LANES), 1)
    low = lane < 2 * nstate
    high = (lane >= 2 * nstate) & (lane < 4 * nstate)

    def split(value):
        top = value.astype(BF16).astype(F32)
        return jnp.where(low, top, jnp.where(high, value - top, 0.0)).astype(BF16)

    def project(u):
        return lax.dot_general(u, wx[...], (((1,), (1,)), ((), ())), preferred_element_type=F32)

    def fill(send, proj):
        send[:, :, pl.ds(0, rank)] = proj[:, :rank].astype(BF16).reshape(nch, part, rank)
        send[:, :, pl.ds(rank, LANES)] = split(proj[:, rank:]).reshape(nch, part, LANES)

    loads[0].wait()
    x2 = x_ref[...].reshape(tokens, width)
    q = lax.broadcasted_iota(jnp.int32, (16, tokens), 0)
    col = lax.broadcasted_iota(jnp.int32, (16, tokens), 1)
    win = q >= 6
    q6 = jnp.where(win, q - 6, q)
    second = q6 >= 3
    tap = jnp.where(second, q6 - 3, q6)
    length = jnp.where(second, len_ref[1], len_ref[0])
    target = jnp.where(win, length - (KCONV - 1) + tap - offset, seq - (KCONV - 1) + tap)
    good = (target >= 0) & (target < seq) & (q < 12)
    place = jnp.where(second, seq, 0) + target
    pick = jnp.where(good & (col == place), 1.0, 0.0).astype(BF16)
    hw[me_ctx] = jnp.dot(pick, x2, preferred_element_type=F32).astype(BF16)
    pl.semaphore_wait(barrier, nctx + nch - 2)
    spread("ctx", lambda to: hw.at[me_ctx], lambda k: hw.at[me_ctx], hw_send, hw_recv)

    sub = lax.broadcasted_iota(jnp.int32, (SEG, width), 0)
    for r in range(nreq):
        xe[r, pl.ds(3 * SEG, seq), :] = jnp.dot(perm, x_ref[r], preferred_element_type=F32)
    loads[1].wait()
    wx[pl.ds(0, rank + 2 * nstate), :] = xw_ref[...]
    wx[pl.ds(rank + 2 * nstate, 2 * nstate), :] = xw_ref[pl.ds(rank, 2 * nstate), :]
    wx[pl.ds(rank + 4 * nstate, LANES - 4 * nstate), :] = jnp.zeros((LANES - 4 * nstate, width), BF16)
    loads[2].wait()
    loads[3].wait()
    cb = cb_ref[...].reshape(1, width)
    for r in range(nreq):
        for k in range(KCONV - 1):
            last = xe[r, pl.ds((nj + k) * SEG, SEG), :]
            xe[r, pl.ds(k * SEG, SEG), :] = jnp.where(sub == 0, 0.0, pltpu.roll(last, 1, 0))
        conv = cb + sum(cw_ref[k : k + 1] * xe[r, pl.ds(k * SEG, seq), :] for k in range(KCONV))
        u_pre[pl.ds(r * seq, seq), :] = silu(conv).astype(BF16).astype(F32)
    fill(send_pre, project(u_pre[...].astype(BF16)))
    spread("ch", lambda to: send_pre.at[to], lambda k: rs_pre.at[k - 1], rsp_send, rsp_recv)

    for load in loads[4:10]:
        load.wait()
    a2[...] = a_ref[...] * (-LOG2E)
    dtb = dtb_ref[...].reshape(1, width)
    skip = skip_ref[...].reshape(1, width)
    for c in range(chunks):
        skips[c : c + 1, :] = skip[:, c * LANES : (c + 1) * LANES]
    req = jnp.broadcast_to(req_ref[...].reshape(1, drows), (drows, drows))
    d0 = lax.broadcasted_iota(jnp.int32, (drows, drows), 0)
    d1 = lax.broadcasted_iota(jnp.int32, (drows, drows), 1)
    request = jnp.sum(jnp.where((d0 == d1) & (req == 1), 1.0, 0.0), axis=1, keepdims=True)
    mask_dec[...] = jnp.broadcast_to(request, (drows, LANES))
    edge_u[...] = jnp.zeros_like(edge_u)

    all_of(hw, nctx, hw_recv)
    before = hw[lax.rem(me_ctx + nctx - 1, nctx)].astype(F32)
    before = jnp.where(me_ctx > 0, before, 0.0)
    edges = KCONV - 1
    for r in range(nreq):
        for k in range(edges):
            own = xe[r, pl.ds(k * SEG, SEG), :]
            xe[r, pl.ds(k * SEG, SEG), :] = jnp.where(sub == 0, row_of(before[3 * r + k : 3 * r + k + 1]), own)
        conv = cb + sum(cw_ref[k : k + 1] * xe[r, pl.ds(k * SEG, edges * SEG), :] for k in range(KCONV))
        u = silu(conv).astype(BF16).astype(F32)
        u_pre[pl.ds(r * seq, edges * SEG), :] = u
        for k in range(edges):
            edge_u[edges * r + k : edges * r + k + 1, :] = u[k * SEG : k * SEG + 1]
    edge_proj = project(edge_u[...].astype(BF16))
    spot = lax.broadcasted_iota(jnp.int32, (16, LANES), 0)
    left = lax.broadcasted_iota(jnp.int32, (16, LANES), 1)
    count = nreq * edges
    maps = jnp.where(left < 2 * nstate, edge_proj[:, rank:], 0.0)
    packed = jnp.where(spot >= 2 * count, pltpu.roll(maps, 2 * count, 0), 0.0)
    wrapped = pltpu.roll(pltpu.roll(maps, 2 * count - 4, 0), 2 * nstate, 1)
    packed = packed + jnp.where((spot >= 2 * count) & (spot < 3 * count - 4), wrapped, 0.0)
    packed = packed + pltpu.roll(packed, LANES // 2, 1)
    coarse = packed.astype(BF16).astype(F32)
    packed = jnp.where(left < LANES // 2, coarse, packed - coarse)
    lower = pltpu.roll(edge_proj[:, LANES:rank], count, 0)
    packed = jnp.where(spot < count, edge_proj[:, :LANES], jnp.where(spot < 2 * count, lower, packed))
    edge[me_ch] = packed.astype(BF16)
    spread("ch", lambda to: edge.at[me_ch], lambda k: edge.at[me_ch], ed_send, ed_recv)

    window = total_of([hw[i].astype(F32) for i in range(nctx)])
    chosen = jnp.broadcast_to(request, (drows, width)) > 0.5
    recent = [
        jnp.where(chosen, row_of(window[9 + k : 10 + k], drows), row_of(window[6 + k : 7 + k], drows))
        for k in range(KCONV - 1)
    ]
    recent = recent + [dx_ref[s].astype(F32) for s in range(steps)]
    for s in range(steps):
        conv = cb + sum(cw_ref[k : k + 1] * recent[s + k] for k in range(KCONV))
        u_dec[pl.ds(s * drows, drows), :] = silu(conv).astype(BF16).astype(F32)
    fill(send_dec, project(u_dec[...].astype(BF16)))
    spread("ch", lambda to: send_dec.at[to], lambda k: rs_dec.at[k - 1], rsd_send, rsd_recv)

    def summed(terms):
        total = total_of(terms)
        tail = total[:, rank:]
        tail = tail + pltpu.roll(tail, 2 * nstate, 1) + pltpu.roll(tail, LANES - 2 * nstate, 1)
        return total[:, :rank].astype(BF16), split(tail)

    def reduce(send, rs, ag, rs_recv, ag_send, ag_recv):
        all_of(rs, nch, rs_recv)
        head, tail = summed([send[me_ch].astype(F32)] + [rs[k].astype(F32) for k in range(nch - 1)])
        ag[me_ch, :, pl.ds(0, rank)] = head
        ag[me_ch, :, pl.ds(rank, LANES)] = tail
        spread("ch", lambda to: ag.at[me_ch], lambda k: ag.at[me_ch], ag_send, ag_recv)

    reduce(send_pre, rs_pre, ag_pre, rsp_recv, agp_send, agp_recv)
    for load in loads[10:]:
        load.wait()
    for r in range(nreq):
        for c in range(chunks):
            g_pre[r * chunks + c] = silu(gate_ref[r, :, c * LANES : (c + 1) * LANES].astype(F32))
    for s in range(steps):
        g_dec[pl.ds(s * drows, drows), :] = silu(dg_ref[s].astype(F32))
    reduce(send_dec, rs_dec, ag_dec, rsd_recv, agd_send, agd_recv)

    w0 = lax.broadcasted_iota(jnp.int32, (LANES, 2 * nstate * LANES), 0)
    w1 = lax.broadcasted_iota(jnp.int32, (LANES, 2 * nstate * LANES), 1) // LANES
    copies = jnp.where((w0 == w1) | (w0 == w1 + 2 * nstate), 1.0, 0.0).astype(BF16)

    def expand(proj, bc, ats):
        for at in ats:
            half = pl.ds(at * nstate * LANES, nstate * LANES)
            own = copies[:, at * nstate * LANES : (at + 1) * nstate * LANES]
            bc[:, half] = jnp.dot(proj[:, rank:], own, preferred_element_type=F32)

    def step_sizes(proj):
        return softplus(jnp.dot(proj[:, :rank], dtw_ref[...], preferred_element_type=F32) + dtb)

    all_of(edge, nch, ed_recv)
    whole = total_of([edge[i].astype(F32) for i in range(nch)])
    maps = whole + pltpu.roll(whole, LANES // 2, 1)
    spread_maps = pltpu.roll(maps, 16 - 2 * count, 0)
    wrapped = pltpu.roll(pltpu.roll(maps, 16 - 2 * count + 4, 0), LANES - 2 * nstate, 1)
    maps = jnp.where(spot < 4, spread_maps, wrapped)
    maps = jnp.where(left < 2 * nstate, maps, pltpu.roll(maps, 2 * nstate, 1))
    fixed = jnp.concatenate(
        [
            whole.astype(BF16).astype(F32),
            pltpu.roll(whole, 16 - count, 0).astype(BF16).astype(F32),
            split(maps).astype(F32),
        ],
        axis=1,
    )
    all_of(ag_pre, nch, agp_recv)
    which = lax.broadcasted_iota(jnp.int32, (part, rank + LANES), 0)
    blocks = []
    for p in range(nch):
        block = ag_pre[p]
        spots = [
            (edges * r + k, r * seq + k * SEG - p * part)
            for r in range(nreq)
            for k in range(edges)
            if 0 <= r * seq + k * SEG - p * part < part
        ]
        for at, spot in spots:
            block = jnp.where(which == spot, row_of(fixed[at : at + 1], part), block.astype(F32)).astype(BF16)
        blocks.append(block)
    proj_pre = jnp.concatenate(blocks, axis=0)

    row = lax.broadcasted_iota(jnp.int32, (seq, 1), 0)
    token = offset + (row % SEG) * nj + row // SEG
    sizes = step_sizes(proj_pre)
    for r in range(nreq):
        own = jnp.where(token < len_ref[r], sizes[r * seq : (r + 1) * seq], 0.0)
        dt_pre[pl.ds(r * seq, seq), :] = own
        whole = jnp.sum(own, axis=0, keepdims=True)
        for c in range(chunks):
            ssum[me_ctx, pl.ds(r * chunks + c, 1), :] = whole[:, c * LANES : (c + 1) * LANES]
    spread("ctx", lambda to: ssum.at[me_ctx], lambda k: ssum.at[me_ctx], ss_send, ss_recv)
    expand(proj_pre, bc_pre, (0,))

    sub1 = lax.broadcasted_iota(jnp.int32, (SEG, LANES), 0)

    def lanes_of(c):
        return pl.ds(pl.multiple_of(c * LANES, LANES), LANES)

    def rates(lanes):
        return [row_of(a2[n : n + 1, lanes]) for n in range(nstate)]

    def of(n):
        return pl.ds(n * LANES, LANES)

    def first_pass(r):
        def body(c, carry):
            rc = r * chunks + c
            lanes = lanes_of(c)
            rate = rates(lanes)
            h = [None] * nstate
            total = None
            for j in range(nj):
                rows = pl.ds(r * seq + j * SEG, SEG)
                dt = dt_pre[rows, lanes]
                dtu = dt * u_pre[rows, lanes]
                total = dt if j == 0 else total + dt
                for n in range(nstate):
                    decay = jnp.exp2(dt * rate[n])
                    d_all[rc, j, n] = decay
                    drive = dtu * bc_pre[rows, of(n)]
                    h[n] = drive if j == 0 else decay * h[n] + drive
            for k in (1, 2, 4):
                for n in range(nstate):
                    h[n] = h[n] + jnp.exp2(rate[n] * total) * jnp.where(sub1 >= k, pltpu.roll(h[n], k, 0), 0.0)
                total = total + jnp.where(sub1 >= k, pltpu.roll(total, k, 0), 0.0)
            for n in range(nstate):
                st32[rc, n : n + 1, :] = h[n][SEG - 1 :]
            states[r, me_ctx, c] = st32[rc].astype(BF16)
            sexcl[rc] = jnp.where(sub1 >= 1, pltpu.roll(total, 1, 0), 0.0)
            for n in range(nstate):
                hexcl[rc, n] = jnp.where(sub1 >= 1, pltpu.roll(h[n], 1, 0), 0.0)
            return carry

        lax.fori_loop(0, chunks, body, 0)
        spread(
            "ctx", lambda to: states.at[r, me_ctx], lambda k: states.at[r, me_ctx], st_send.at[r], st_recv.at[r]
        )

    for r in range(nreq):
        first_pass(r)

    expand(proj_pre, bc_pre, (1,))

    all_of(ag_dec, nch, agd_recv)
    proj_dec = ag_dec[...].reshape(nch * part, rank + LANES)
    dt_dec[...] = step_sizes(proj_dec)
    expand(proj_dec, bc_dec, (0, 1))

    def decode_local(gc, carry):
        g, c = gc // chunks, gc % chunks
        lanes = lanes_of(c)
        rate = rates(lanes)
        skipping = row_of(skips[pl.ds(c, 1), :])
        h, product = [None] * nstate, [None] * nstate
        for s in range(steps):
            rows = pl.ds(pl.multiple_of(s * drows + g * SEG, SEG), SEG)
            dt = dt_dec[rows, lanes]
            u = u_dec[rows, lanes]
            dtu = dt * u
            terms = [skipping * u]
            for n in range(nstate):
                decay = jnp.exp2(dt * rate[n])
                cout = bc_dec[rows, of(nstate + n)]
                drive = dtu * bc_dec[rows, of(n)]
                h[n] = drive if s == 0 else decay * h[n] + drive
                product[n] = decay if s == 0 else decay * product[n]
                terms.append(cout * h[n])
                e_dec[gc, s, n] = cout * product[n]
            y_dec[rows, lanes] = total_of(terms)
        return carry

    lax.fori_loop(0, groups * chunks, decode_local, 0)

    def prefill_local(rc, carry):
        r, c = rc // chunks, rc % chunks
        lanes = lanes_of(c)
        skipping = row_of(skips[pl.ds(c, 1), :])
        h = [hexcl[rc, n] for n in range(nstate)]
        for n in range(nstate):
            pseg[rc, n] = jnp.exp2(row_of(a2[n : n + 1, lanes]) * sexcl[rc])
        product = [None] * nstate
        for j in range(nj):
            rows = pl.ds(pl.multiple_of(r * seq + j * SEG, SEG), SEG)
            u = u_pre[rows, lanes]
            dtu = dt_pre[rows, lanes] * u
            terms = [skipping * u]
            for n in range(nstate):
                decay = d_all[rc, j, n]
                cout = bc_pre[rows, of(nstate + n)]
                h[n] = decay * h[n] + dtu * bc_pre[rows, of(n)]
                product[n] = decay if j == 0 else decay * product[n]
                terms.append(cout * h[n])
                e_pre[rc, j, n] = cout * product[n]
            y_loc[rc, j] = total_of(terms)
        return carry

    lax.fori_loop(0, nrc, prefill_local, 0)

    all_of(ssum, nctx, ss_recv)
    for rc in range(nrc):
        rate = a2[:, (rc % chunks) * LANES : (rc % chunks + 1) * LANES]
        for i in range(nctx):
            weight[rc, i] = jnp.exp2(rate * row_of(ssum[i, rc : rc + 1, :], nstate))

    for r in range(nreq):
        all_of(states.at[r], nctx, st_recv.at[r])
        for c in range(chunks):
            rc = r * chunks + c
            h = jnp.zeros((nstate, LANES), F32)
            for i in range(nctx):
                prefix[rc, i] = h
                h = weight[rc, i] * h + states[r, i, c].astype(F32)
            prefix[rc, nctx] = h

    def prefill_rest(rc, carry):
        h = [pseg[rc, n] * row_of(prefix[rc, me_ctx, n : n + 1, :]) for n in range(nstate)]
        for j in range(nj):
            y = total_of([y_loc[rc, j]] + [e_pre[rc, j, n] * h[n] for n in range(nstate)])
            y_nat[rc, pl.ds(j, SEG, stride=nj), :] = y
        return carry

    lax.fori_loop(0, nrc, prefill_rest, 0)

    def decode_rest(c, carry):
        lanes = lanes_of(c)
        half = nstate // 2
        for first in (0, half):
            at = range(first, first + half)
            f0 = [row_of(prefix[c, nctx, n : n + 1, :]) for n in at]
            f1 = [row_of(prefix[chunks + c, nctx, n : n + 1, :]) for n in at]
            for g in range(groups):
                mine = mask_dec[g * SEG : (g + 1) * SEG, :] > 0.5
                h = [jnp.where(mine, b, a) for a, b in zip(f0, f1)]
                for s in range(steps):
                    rows = pl.ds(s * drows + g * SEG, SEG)
                    terms = [e_dec[g * chunks + c, s, n] * h[n - first] for n in at]
                    if first == 0:
                        y_half[rows, lanes] = total_of(terms + [y_dec[rows, lanes]])
                    else:
                        y_fin[rows, lanes] = total_of(terms + [y_half[rows, lanes]]) * g_dec[rows, lanes]
        return carry

    lax.fori_loop(0, chunks, decode_rest, 0)

    natural = offset + lax.broadcasted_iota(jnp.int32, (seq, 1), 0)
    for r in range(nreq):
        live = natural < len_ref[r]
        for c in range(chunks):
            y = y_nat[r * chunks + c] * g_pre[r * chunks + c]
            out_ref[r, :, pl.ds(c * LANES, LANES)] = jnp.where(live, y, 0.0).astype(BF16)
    for s in range(steps):
        dout_ref[s] = y_fin[pl.ds(s * drows, drows), :].astype(BF16)

    all_of(hw, nctx, hw_send)
    all_of(edge, nch, ed_send)
    all_of(rs_pre, nch, rsp_send)
    all_of(rs_dec, nch, rsd_send)
    all_of(ag_pre, nch, agp_send)
    all_of(ag_dec, nch, agd_send)
    all_of(ssum, nctx, ss_send)
    for r in range(nreq):
        all_of(states.at[r], nctx, st_send.at[r])


def on_device(nctx, nch, *args):
    args = list(args)
    args[4] = args[4].T
    inputs, dt_weight, decay_rate, row_request, dec_inputs = args[0], args[5], args[7], args[10], args[11]
    nreq, seq, width = inputs.shape
    steps, drows = dec_inputs.shape[:2]
    rank, nstate = dt_weight.shape[0], decay_rate.shape[0]
    tokens, dtokens = nreq * seq, steps * drows
    nj, chunks, groups = seq // SEG, width // LANES, drows // SEG
    nrc = nreq * chunks
    cols = rank + LANES
    part, dpart = tokens // nch, dtokens // nch
    hbm = pl.BlockSpec(memory_space=pl.ANY)
    vmem = pl.BlockSpec(memory_space=pltpu.VMEM)
    smem = pl.BlockSpec(memory_space=pltpu.SMEM)
    sem = pltpu.SemaphoreType.DMA
    scratch = [pltpu.VMEM(a.shape, a.dtype) for i, a in enumerate(args) if i != 9] + [
        pltpu.VMEM((nctx, 16, width), BF16),
        pltpu.VMEM((nreq, (nj + KCONV - 1) * SEG, width), F32),
        pltpu.VMEM((tokens, width), F32),
        pltpu.VMEM((dtokens, width), F32),
        pltpu.VMEM((16, width), F32),
        pltpu.VMEM((nch, 16, LANES), BF16),
        pltpu.VMEM((nch, part, cols), BF16),
        pltpu.VMEM((nch, dpart, cols), BF16),
        pltpu.VMEM((nch - 1, part, cols), BF16),
        pltpu.VMEM((nch - 1, dpart, cols), BF16),
        pltpu.VMEM((nch, part, cols), BF16),
        pltpu.VMEM((nch, dpart, cols), BF16),
        pltpu.VMEM((cols, width), BF16),
        pltpu.VMEM((nstate, width), F32),
        pltpu.VMEM((8, LANES), F32),
        pltpu.VMEM((tokens, width), F32),
        pltpu.VMEM((dtokens, width), F32),
        pltpu.VMEM((tokens, 2 * nstate * LANES), F32),
        pltpu.VMEM((dtokens, 2 * nstate * LANES), F32),
        pltpu.VMEM((nrc, nj, nstate, SEG, LANES), F32),
        pltpu.VMEM((nrc, nj, nstate, SEG, LANES), F32),
        pltpu.VMEM((groups * chunks, steps, nstate, SEG, LANES), F32),
        pltpu.VMEM((nctx, nrc, LANES), F32),
        pltpu.VMEM((nrc, nstate, LANES), F32),
        pltpu.VMEM((nreq, nctx, chunks, nstate, LANES), BF16),
        pltpu.VMEM((nrc, nstate, SEG, LANES), F32),
        pltpu.VMEM((nrc, SEG, LANES), F32),
        pltpu.VMEM((nrc, nstate, SEG, LANES), F32),
        pltpu.VMEM((nrc, nctx, nstate, LANES), F32),
        pltpu.VMEM((nrc, nctx + 1, nstate, LANES), F32),
        pltpu.VMEM((nrc, nj, SEG, LANES), F32),
        pltpu.VMEM((nrc, seq, LANES), F32),
        pltpu.VMEM((dtokens, width), F32),
        pltpu.VMEM((dtokens, width), F32),
        pltpu.VMEM((dtokens, width), F32),
        pltpu.VMEM((nrc, seq, LANES), F32),
        pltpu.VMEM((dtokens, width), F32),
        pltpu.VMEM((drows, LANES), F32),
        sem((len(args) - 1,)),
    ] + [sem] * 14 + [sem((nreq,))] * 2
    shapes = (jax.ShapeDtypeStruct(inputs.shape, BF16), jax.ShapeDtypeStruct(dec_inputs.shape, BF16))
    return pl.pallas_call(
        functools.partial(kernel, nctx, nch),
        out_shape=tuple(pltpu.VMEM(s.shape, s.dtype) for s in shapes),
        in_specs=[hbm] * 9 + [smem] + [hbm] * 3,
        out_specs=(vmem, vmem),
        scratch_shapes=scratch,
        compiler_params=pltpu.CompilerParams(
            collective_id=0, has_side_effects=True, vmem_limit_bytes=65011712 + 1536 * 1024 - 64 * 1024
        ),
    )(*args)


def solution(mesh):
    placed = (
        P(None, "ctx", "ch"),
        P(None, "ctx", "ch"),
        P(None, "ch"),
        P("ch"),
        P("ch", None),
        P(None, "ch"),
        P("ch"),
        P(None, "ch"),
        P("ch"),
        P(),
        P("ctx"),
        P(None, "ctx", "ch"),
        P(None, "ctx", "ch"),
    )
    return jax.shard_map(
        functools.partial(on_device, mesh.shape["ctx"], mesh.shape["ch"]),
        mesh=mesh,
        in_specs=placed,
        out_specs=(P(None, "ctx", "ch"), P(None, "ctx", "ch")),
        check_vma=False,
    )
```

```python
import functools
import math

import jax
import jax.numpy as jnp
from jax import lax
from jax.experimental import pallas as pl
from jax.experimental.pallas import tpu as pltpu
from jax.sharding import PartitionSpec as P

MESH = pl.DeviceIdType.MESH
F32 = jnp.float32
BF16 = jnp.bfloat16
LOG2E = math.log2(math.e)
KCONV = 4
SEG = 8
LANES = 128
SIDE = 4


def softplus(x):
    return jnp.maximum(x, 0.0) + jnp.log1p(jnp.exp(-jnp.abs(x)))


def silu(x):
    return x / (1.0 + jnp.exp(-x))


def row_of(value, rows=SEG):
    return jnp.broadcast_to(value, (rows, value.shape[1]))


def total_of(terms):
    while len(terms) > 1:
        terms = [a + b for a, b in zip(terms[::2], terms[1::2])] + ([terms[-1]] if len(terms) % 2 else [])
    return terms[0]


def ring(d):
    return min(d, SIDE - d)


def kernel(
    nctx, nch,
    x_hbm, gate_hbm, cw_hbm, cb_hbm, xw_hbm, dtw_hbm, dtb_hbm, a_hbm, skip_hbm, len_ref, req_hbm, dx_hbm, dg_hbm,
    out_ref, dout_ref,
    x_ref, gate_ref, cw_ref, cb_ref, xw_ref, dtw_ref, dtb_ref, a_ref, skip_ref, req_ref, dx_ref, dg_ref,
    hw, xe, u_pre, u_dec, edge_u, edge, send_pre, send_dec, rs_pre, rs_dec, ag_pre, ag_dec, wx, a2, a2b, skips,
    dt_pre, dt_dec, bc_pre, bc_dec, d_all, e_pre, e_dec, ssum, st32, states, hexcl, sexcl, pseg, weight, prefix,
    y_loc, y_nat, y_dec, y_half, y_fin, g_pre, g_dec, mask_dec,
    in_sems, hw_send, hw_recv, ed_send, ed_recv, rsp_send, rsp_recv, rsd_send, rsd_recv,
    agp_send, agp_recv, agd_send, agd_recv, ss_send, ss_recv, st_send, st_recv,
):
    nreq, seq, width = x_ref.shape
    steps, drows = dx_ref.shape[0], dx_ref.shape[1]
    nstate = a_ref.shape[0]
    rank = dtw_ref.shape[0]
    tokens = nreq * seq
    nj = seq // SEG
    chunks = width // LANES
    nrc = nreq * chunks
    groups = drows // SEG
    part = tokens // nch
    me_ctx = lax.axis_index("ctx")
    me_ch = lax.axis_index("ch")
    offset = me_ctx * seq

    pairs = [
        (x_hbm, x_ref), (xw_hbm, xw_ref), (cw_hbm, cw_ref), (cb_hbm, cb_ref), (dx_hbm, dx_ref), (req_hbm, req_ref),
        (dtw_hbm, dtw_ref), (dtb_hbm, dtb_ref), (a_hbm, a_ref), (skip_hbm, skip_ref), (gate_hbm, gate_ref),
        (dg_hbm, dg_ref),
    ]
    loads = []
    for i, (src, dst) in enumerate(pairs):
        sem = in_sems.at[i]
        if len(dst.shape) == 3:
            pieces = [(src.at[k], dst.at[k]) for k in range(dst.shape[0])]
        else:
            pieces = [(src, dst)]
        if i == 0:
            half = pl.ds(0, seq // 2), pl.ds(seq // 2, seq // 2)
            pieces = [(a.at[rows], b.at[rows]) for a, b in pieces for rows in half]
        loads.append((pltpu.make_async_copy(src, dst, sem), [pltpu.make_async_copy(a, b, sem) for a, b in pieces]))

    def begin(some):
        for load, pieces in some:
            for piece in pieces:
                piece.start()

    begin(loads[:4])

    def far_ch():
        for k in sorted(range(1, nch), key=lambda k: -(ring(k // SIDE) + ring(k % SIDE))):
            y = lax.rem(me_ch // SIDE + k // SIDE, nch // SIDE)
            z = lax.rem(lax.rem(me_ch, SIDE) + k % SIDE, SIDE)
            yield k, y * SIDE + z

    def far_ctx():
        for k in sorted(range(1, nctx), key=lambda k: -ring(k // 2)):
            x = lax.rem(me_ctx // 2 + k // 2, nctx // 2)
            core = lax.rem(lax.rem(me_ctx, 2) + k % 2, 2)
            yield k, x * 2 + core

    far = {"ch": far_ch, "ctx": far_ctx}

    barrier = pltpu.get_barrier_semaphore()
    for axis in ("ch", "ctx"):
        for k, to in far[axis]():
            pl.semaphore_signal(barrier, inc=1, device_id={axis: to}, device_id_type=MESH)

    begin(loads[4:])

    def spread(axis, src, dst, send_sem, recv_sem):
        for k, to in far[axis]():
            pltpu.make_async_remote_copy(
                src_ref=src(to), dst_ref=dst(k), send_sem=send_sem, recv_sem=recv_sem,
                device_id={axis: to}, device_id_type=MESH,
            ).start()

    def all_of(ref, count, sem):
        view = ref.at[pl.ds(0, count - 1)]
        pltpu.make_async_copy(view, view, sem).wait()

    i0 = lax.broadcasted_iota(jnp.int32, (seq, seq), 0)
    i1 = lax.broadcasted_iota(jnp.int32, (seq, seq), 1)
    perm = jnp.where(i1 == (i0 % SEG) * nj + i0 // SEG, 1.0, 0.0).astype(BF16)
    lane = lax.broadcasted_iota(jnp.int32, (1, LANES), 1)
    low = lane < 2 * nstate
    high = (lane >= 2 * nstate) & (lane < 4 * nstate)

    def split(value):
        top = value.astype(BF16).astype(F32)
        return jnp.where(low, top, jnp.where(high, value - top, 0.0)).astype(BF16)

    def project(u):
        return lax.dot_general(u, wx[...], (((1,), (1,)), ((), ())), preferred_element_type=F32)

    def fill(send, proj):
        send[:, :, pl.ds(0, rank)] = proj[:, :rank].astype(BF16).reshape(nch, part, rank)
        send[:, :, pl.ds(rank, LANES)] = split(proj[:, rank:]).reshape(nch, part, LANES)

    loads[0][0].wait()
    x2 = x_ref[...].reshape(tokens, width)
    q = lax.broadcasted_iota(jnp.int32, (16, tokens), 0)
    col = lax.broadcasted_iota(jnp.int32, (16, tokens), 1)
    win = q >= 6
    q6 = jnp.where(win, q - 6, q)
    second = q6 >= 3
    tap = jnp.where(second, q6 - 3, q6)
    length = jnp.where(second, len_ref[1], len_ref[0])
    target = jnp.where(win, length - (KCONV - 1) + tap - offset, seq - (KCONV - 1) + tap)
    good = (target >= 0) & (target < seq) & (q < 12)
    place = jnp.where(second, seq, 0) + target
    pick = jnp.where(good & (col == place), 1.0, 0.0).astype(BF16)
    hw[me_ctx] = jnp.dot(pick, x2, preferred_element_type=F32).astype(BF16)
    pl.semaphore_wait(barrier, nctx + nch - 2)
    spread("ctx", lambda to: hw.at[me_ctx], lambda k: hw.at[me_ctx], hw_send, hw_recv)

    sub = lax.broadcasted_iota(jnp.int32, (SEG, width), 0)
    for r in range(nreq):
        xe[r, pl.ds(3 * SEG, seq), :] = jnp.dot(perm, x_ref[r], preferred_element_type=F32)
    loads[1][0].wait()
    wx[pl.ds(0, rank + 2 * nstate), :] = xw_ref[...]
    wx[pl.ds(rank + 2 * nstate, 2 * nstate), :] = xw_ref[pl.ds(rank, 2 * nstate), :]
    wx[pl.ds(rank + 4 * nstate, LANES - 4 * nstate), :] = jnp.zeros((LANES - 4 * nstate, width), BF16)
    loads[2][0].wait()
    loads[3][0].wait()
    cb = cb_ref[...].reshape(1, width)
    for r in range(nreq):
        for k in range(KCONV - 1):
            last = xe[r, pl.ds((nj + k) * SEG, SEG), :]
            xe[r, pl.ds(k * SEG, SEG), :] = jnp.where(sub == 0, 0.0, pltpu.roll(last, 1, 0))
        conv = cb + sum(cw_ref[k : k + 1] * xe[r, pl.ds(k * SEG, seq), :] for k in range(KCONV))
        u_pre[pl.ds(r * seq, seq), :] = silu(conv).astype(BF16).astype(F32)
    fill(send_pre, project(u_pre[...].astype(BF16)))
    spread("ch", lambda to: send_pre.at[to], lambda k: rs_pre.at[k - 1], rsp_send, rsp_recv)

    for load, _ in loads[4:10]:
        load.wait()
    a2[...] = a_ref[...] * (-LOG2E)
    for c in range(chunks):
        for n in range(nstate):
            a2b[c, n] = row_of(a2[n : n + 1, c * LANES : (c + 1) * LANES])
    dtb = dtb_ref[...].reshape(1, width)
    skip = skip_ref[...].reshape(1, width)
    for c in range(chunks):
        skips[c : c + 1, :] = skip[:, c * LANES : (c + 1) * LANES]
    req = jnp.broadcast_to(req_ref[...].reshape(1, drows), (drows, drows))
    d0 = lax.broadcasted_iota(jnp.int32, (drows, drows), 0)
    d1 = lax.broadcasted_iota(jnp.int32, (drows, drows), 1)
    request = jnp.sum(jnp.where((d0 == d1) & (req == 1), 1.0, 0.0), axis=1, keepdims=True)
    mask_dec[...] = jnp.broadcast_to(request, (drows, LANES))
    edge_u[...] = jnp.zeros_like(edge_u)

    all_of(hw, nctx, hw_recv)
    before = hw[lax.rem(me_ctx + nctx - 1, nctx)].astype(F32)
    before = jnp.where(me_ctx > 0, before, 0.0)
    edges = KCONV - 1
    for r in range(nreq):
        for k in range(edges):
            own = xe[r, pl.ds(k * SEG, SEG), :]
            xe[r, pl.ds(k * SEG, SEG), :] = jnp.where(sub == 0, row_of(before[3 * r + k : 3 * r + k + 1]), own)
        conv = cb + sum(cw_ref[k : k + 1] * xe[r, pl.ds(k * SEG, edges * SEG), :] for k in range(KCONV))
        u = silu(conv).astype(BF16).astype(F32)
        u_pre[pl.ds(r * seq, edges * SEG), :] = u
        for k in range(edges):
            edge_u[edges * r + k : edges * r + k + 1, :] = u[k * SEG : k * SEG + 1]
    edge_proj = project(edge_u[...].astype(BF16))
    spot = lax.broadcasted_iota(jnp.int32, (16, LANES), 0)
    left = lax.broadcasted_iota(jnp.int32, (16, LANES), 1)
    count = nreq * edges
    maps = jnp.where(left < 2 * nstate, edge_proj[:, rank:], 0.0)
    packed = jnp.where(spot >= 2 * count, pltpu.roll(maps, 2 * count, 0), 0.0)
    wrapped = pltpu.roll(pltpu.roll(maps, 2 * count - 4, 0), 2 * nstate, 1)
    packed = packed + jnp.where((spot >= 2 * count) & (spot < 3 * count - 4), wrapped, 0.0)
    packed = packed + pltpu.roll(packed, LANES // 2, 1)
    coarse = packed.astype(BF16).astype(F32)
    packed = jnp.where(left < LANES // 2, coarse, packed - coarse)
    lower = pltpu.roll(edge_proj[:, LANES:rank], count, 0)
    packed = jnp.where(spot < count, edge_proj[:, :LANES], jnp.where(spot < 2 * count, lower, packed))
    edge[me_ch] = packed.astype(BF16)
    spread("ch", lambda to: edge.at[me_ch], lambda k: edge.at[me_ch], ed_send, ed_recv)

    window = total_of([hw[i].astype(F32) for i in range(nctx)])
    chosen = jnp.broadcast_to(request, (drows, width)) > 0.5
    recent = [
        jnp.where(chosen, row_of(window[9 + k : 10 + k], drows), row_of(window[6 + k : 7 + k], drows))
        for k in range(KCONV - 1)
    ]
    recent = recent + [dx_ref[s].astype(F32) for s in range(steps)]
    for s in range(steps):
        conv = cb + sum(cw_ref[k : k + 1] * recent[s + k] for k in range(KCONV))
        u_dec[pl.ds(s * drows, drows), :] = silu(conv).astype(BF16).astype(F32)
    fill(send_dec, project(u_dec[...].astype(BF16)))
    spread("ch", lambda to: send_dec.at[to], lambda k: rs_dec.at[k - 1], rsd_send, rsd_recv)

    def summed(terms):
        total = total_of(terms)
        tail = total[:, rank:]
        tail = tail + pltpu.roll(tail, 2 * nstate, 1) + pltpu.roll(tail, LANES - 2 * nstate, 1)
        return total[:, :rank].astype(BF16), split(tail)

    def reduce(send, rs, ag, rs_recv, ag_send, ag_recv):
        all_of(rs, nch, rs_recv)
        head, tail = summed([send[me_ch].astype(F32)] + [rs[k].astype(F32) for k in range(nch - 1)])
        ag[me_ch, :, pl.ds(0, rank)] = head
        ag[me_ch, :, pl.ds(rank, LANES)] = tail
        spread("ch", lambda to: ag.at[me_ch], lambda k: ag.at[me_ch], ag_send, ag_recv)

    reduce(send_pre, rs_pre, ag_pre, rsp_recv, agp_send, agp_recv)
    for load, _ in loads[10:]:
        load.wait()
    for r in range(nreq):
        for c in range(chunks):
            g_pre[r * chunks + c] = silu(gate_ref[r, :, c * LANES : (c + 1) * LANES].astype(F32))
    for s in range(steps):
        g_dec[pl.ds(s * drows, drows), :] = silu(dg_ref[s].astype(F32))
    reduce(send_dec, rs_dec, ag_dec, rsd_recv, agd_send, agd_recv)

    w0 = lax.broadcasted_iota(jnp.int32, (LANES, 2 * nstate * LANES), 0)
    w1 = lax.broadcasted_iota(jnp.int32, (LANES, 2 * nstate * LANES), 1) // LANES
    copies = jnp.where((w0 == w1) | (w0 == w1 + 2 * nstate), 1.0, 0.0).astype(BF16)

    def expand(proj, bc, ats):
        for at in ats:
            half = pl.ds(at * nstate * LANES, nstate * LANES)
            own = copies[:, at * nstate * LANES : (at + 1) * nstate * LANES]
            bc[:, half] = jnp.dot(proj[:, rank:], own, preferred_element_type=F32)

    def step_sizes(proj):
        return softplus(jnp.dot(proj[:, :rank], dtw_ref[...], preferred_element_type=F32) + dtb)

    all_of(edge, nch, ed_recv)
    whole = total_of([edge[i].astype(F32) for i in range(nch)])
    maps = whole + pltpu.roll(whole, LANES // 2, 1)
    spread_maps = pltpu.roll(maps, 16 - 2 * count, 0)
    wrapped = pltpu.roll(pltpu.roll(maps, 16 - 2 * count + 4, 0), LANES - 2 * nstate, 1)
    maps = jnp.where(spot < 4, spread_maps, wrapped)
    maps = jnp.where(left < 2 * nstate, maps, pltpu.roll(maps, 2 * nstate, 1))
    fixed = jnp.concatenate(
        [
            whole.astype(BF16).astype(F32),
            pltpu.roll(whole, 16 - count, 0).astype(BF16).astype(F32),
            split(maps).astype(F32),
        ],
        axis=1,
    )
    all_of(ag_pre, nch, agp_recv)
    which = lax.broadcasted_iota(jnp.int32, (part, rank + LANES), 0)
    blocks = []
    for p in range(nch):
        block = ag_pre[p]
        spots = [
            (edges * r + k, r * seq + k * SEG - p * part)
            for r in range(nreq)
            for k in range(edges)
            if 0 <= r * seq + k * SEG - p * part < part
        ]
        for at, spot in spots:
            block = jnp.where(which == spot, row_of(fixed[at : at + 1], part), block.astype(F32)).astype(BF16)
        blocks.append(block)
    proj_pre = jnp.concatenate(blocks, axis=0)

    row = lax.broadcasted_iota(jnp.int32, (seq, 1), 0)
    token = offset + (row % SEG) * nj + row // SEG
    sizes = step_sizes(proj_pre)
    for r in range(nreq):
        own = jnp.where(token < len_ref[r], sizes[r * seq : (r + 1) * seq], 0.0)
        dt_pre[pl.ds(r * seq, seq), :] = own
        whole = jnp.sum(own, axis=0, keepdims=True)
        for c in range(chunks):
            ssum[me_ctx, pl.ds(r * chunks + c, 1), :] = whole[:, c * LANES : (c + 1) * LANES]
    spread("ctx", lambda to: ssum.at[me_ctx], lambda k: ssum.at[me_ctx], ss_send, ss_recv)
    expand(proj_pre, bc_pre, (0,))

    sub1 = lax.broadcasted_iota(jnp.int32, (SEG, LANES), 0)

    def lanes_of(c):
        return pl.ds(pl.multiple_of(c * LANES, LANES), LANES)

    def rates(c):
        return [a2b[c, n] for n in range(nstate)]

    def of(n):
        return pl.ds(n * LANES, LANES)

    def first_pass(r):
        def body(c, carry):
            rc = r * chunks + c
            lanes = lanes_of(c)
            rate = rates(c)
            h = [None] * nstate
            total = None
            for j in range(nj):
                rows = pl.ds(r * seq + j * SEG, SEG)
                dt = dt_pre[rows, lanes]
                dtu = dt * u_pre[rows, lanes]
                total = dt if j == 0 else total + dt
                for n in range(nstate):
                    decay = jnp.exp2(dt * rate[n])
                    d_all[rc, j, n] = decay
                    drive = dtu * bc_pre[rows, of(n)]
                    h[n] = drive if j == 0 else decay * h[n] + drive
            for k in (1, 2, 4):
                for n in range(nstate):
                    h[n] = h[n] + jnp.exp2(rate[n] * total) * jnp.where(sub1 >= k, pltpu.roll(h[n], k, 0), 0.0)
                total = total + jnp.where(sub1 >= k, pltpu.roll(total, k, 0), 0.0)
            for n in range(nstate):
                st32[rc, n : n + 1, :] = h[n][SEG - 1 :]
            states[r, me_ctx, c] = st32[rc].astype(BF16)
            sexcl[rc] = jnp.where(sub1 >= 1, pltpu.roll(total, 1, 0), 0.0)
            for n in range(nstate):
                hexcl[rc, n] = jnp.where(sub1 >= 1, pltpu.roll(h[n], 1, 0), 0.0)
            return carry

        for first in range(0, chunks, 2):
            lax.fori_loop(first, first + 2, body, 0)
            own = states.at[r, me_ctx, pl.ds(first, 2)]
            spread("ctx", lambda to: own, lambda k: own, st_send.at[r], st_recv.at[r])

    for r in range(nreq):
        first_pass(r)

    expand(proj_pre, bc_pre, (1,))

    all_of(ag_dec, nch, agd_recv)
    proj_dec = ag_dec[...].reshape(nch * part, rank + LANES)
    dt_dec[...] = step_sizes(proj_dec)
    expand(proj_dec, bc_dec, (0, 1))

    def decode_local(c, carry):
        lanes = lanes_of(c)
        rate = rates(c)
        skipping = row_of(skips[pl.ds(c, 1), :])

        def group(g, carry):
            h, product = [None] * nstate, [None] * nstate
            for s in range(steps):
                rows = pl.ds(pl.multiple_of(s * drows + g * SEG, SEG), SEG)
                dt = dt_dec[rows, lanes]
                u = u_dec[rows, lanes]
                dtu = dt * u
                terms = [skipping * u]
                for n in range(nstate):
                    decay = jnp.exp2(dt * rate[n])
                    cout = bc_dec[rows, of(nstate + n)]
                    drive = dtu * bc_dec[rows, of(n)]
                    h[n] = drive if s == 0 else decay * h[n] + drive
                    product[n] = decay if s == 0 else decay * product[n]
                    terms.append(cout * h[n])
                    e_dec[g * chunks + c, s, n] = cout * product[n]
                y_dec[rows, lanes] = total_of(terms)
            return carry

        return lax.fori_loop(0, groups, group, carry, unroll=4)

    lax.fori_loop(0, chunks, decode_local, 0)

    all_of(ssum, nctx, ss_recv)
    for rc in range(nrc):
        rate = a2[:, (rc % chunks) * LANES : (rc % chunks + 1) * LANES]
        for i in range(nctx):
            weight[rc, i] = jnp.exp2(rate * row_of(ssum[i, rc : rc + 1, :], nstate))

    for r in range(nreq):
        all_of(states.at[r], nctx, st_recv.at[r])
        for c in range(chunks):
            rc = r * chunks + c
            h = jnp.zeros((nstate, LANES), F32)
            for i in range(nctx):
                prefix[rc, i] = h
                h = weight[rc, i] * h + states[r, i, c].astype(F32)
            prefix[rc, nctx] = h

    def prefill_states(rc, carry):
        r, c = rc // chunks, rc % chunks
        lanes = lanes_of(c)
        skipping = row_of(skips[pl.ds(c, 1), :])
        start = sexcl[rc]
        h = [
            hexcl[rc, n]
            + jnp.exp2(a2b[c, n] * start) * row_of(prefix[rc, me_ctx, n : n + 1, :])
            for n in range(nstate)
        ]
        for j in range(nj):
            rows = pl.ds(pl.multiple_of(r * seq + j * SEG, SEG), SEG)
            u = u_pre[rows, lanes]
            dtu = dt_pre[rows, lanes] * u
            terms = [skipping * u]
            for n in range(nstate):
                h[n] = d_all[rc, j, n] * h[n] + dtu * bc_pre[rows, of(n)]
                terms.append(bc_pre[rows, of(nstate + n)] * h[n])
            y_nat[rc, pl.ds(j, SEG, stride=nj), :] = total_of(terms)
        return carry

    lax.fori_loop(0, nrc, prefill_states, 0)

    def decode_rest(c, carry):
        lanes = lanes_of(c)
        half = nstate // 2
        for first in (0, half):
            at = range(first, first + half)
            f0 = [row_of(prefix[c, nctx, n : n + 1, :]) for n in at]
            f1 = [row_of(prefix[chunks + c, nctx, n : n + 1, :]) for n in at]
            for g in range(groups):
                mine = mask_dec[g * SEG : (g + 1) * SEG, :] > 0.5
                h = [jnp.where(mine, b, a) for a, b in zip(f0, f1)]
                for s in range(steps):
                    rows = pl.ds(s * drows + g * SEG, SEG)
                    terms = [e_dec[g * chunks + c, s, n] * h[n - first] for n in at]
                    if first == 0:
                        y_half[rows, lanes] = total_of(terms + [y_dec[rows, lanes]])
                    else:
                        y_fin[rows, lanes] = total_of(terms + [y_half[rows, lanes]]) * g_dec[rows, lanes]
        return carry

    lax.fori_loop(0, chunks, decode_rest, 0)

    natural = offset + lax.broadcasted_iota(jnp.int32, (seq, 1), 0)
    for r in range(nreq):
        live = natural < len_ref[r]
        for c in range(chunks):
            y = y_nat[r * chunks + c] * g_pre[r * chunks + c]
            out_ref[r, :, pl.ds(c * LANES, LANES)] = jnp.where(live, y, 0.0).astype(BF16)
    for s in range(steps):
        dout_ref[s] = y_fin[pl.ds(s * drows, drows), :].astype(BF16)

    all_of(hw, nctx, hw_send)
    all_of(edge, nch, ed_send)
    all_of(rs_pre, nch, rsp_send)
    all_of(rs_dec, nch, rsd_send)
    all_of(ag_pre, nch, agp_send)
    all_of(ag_dec, nch, agd_send)
    all_of(ssum, nctx, ss_send)
    for r in range(nreq):
        all_of(states.at[r], nctx, st_send.at[r])


def on_device(nctx, nch, *args):
    args = list(args)
    args[4] = args[4].T
    inputs, dt_weight, decay_rate, row_request, dec_inputs = args[0], args[5], args[7], args[10], args[11]
    nreq, seq, width = inputs.shape
    steps, drows = dec_inputs.shape[:2]
    rank, nstate = dt_weight.shape[0], decay_rate.shape[0]
    tokens, dtokens = nreq * seq, steps * drows
    nj, chunks, groups = seq // SEG, width // LANES, drows // SEG
    nrc = nreq * chunks
    cols = rank + LANES
    part, dpart = tokens // nch, dtokens // nch
    hbm = pl.BlockSpec(memory_space=pl.ANY)
    vmem = pl.BlockSpec(memory_space=pltpu.VMEM)
    smem = pl.BlockSpec(memory_space=pltpu.SMEM)
    sem = pltpu.SemaphoreType.DMA
    scratch = [pltpu.VMEM(a.shape, a.dtype) for i, a in enumerate(args) if i != 9] + [
        pltpu.VMEM((nctx, 16, width), BF16),
        pltpu.VMEM((nreq, (nj + KCONV - 1) * SEG, width), F32),
        pltpu.VMEM((tokens, width), F32),
        pltpu.VMEM((dtokens, width), F32),
        pltpu.VMEM((16, width), F32),
        pltpu.VMEM((nch, 16, LANES), BF16),
        pltpu.VMEM((nch, part, cols), BF16),
        pltpu.VMEM((nch, dpart, cols), BF16),
        pltpu.VMEM((nch - 1, part, cols), BF16),
        pltpu.VMEM((nch - 1, dpart, cols), BF16),
        pltpu.VMEM((nch, part, cols), BF16),
        pltpu.VMEM((nch, dpart, cols), BF16),
        pltpu.VMEM((cols, width), BF16),
        pltpu.VMEM((nstate, width), F32),
        pltpu.VMEM((chunks, nstate, SEG, LANES), F32),
        pltpu.VMEM((8, LANES), F32),
        pltpu.VMEM((tokens, width), F32),
        pltpu.VMEM((dtokens, width), F32),
        pltpu.VMEM((tokens, 2 * nstate * LANES), F32),
        pltpu.VMEM((dtokens, 2 * nstate * LANES), F32),
        pltpu.VMEM((nrc, nj, nstate, SEG, LANES), F32),
        pltpu.VMEM((nrc, nj, nstate, SEG, LANES), F32),
        pltpu.VMEM((groups * chunks, steps, nstate, SEG, LANES), F32),
        pltpu.VMEM((nctx, nrc, LANES), F32),
        pltpu.VMEM((nrc, nstate, LANES), F32),
        pltpu.VMEM((nreq, nctx, chunks, nstate, LANES), BF16),
        pltpu.VMEM((nrc, nstate, SEG, LANES), F32),
        pltpu.VMEM((nrc, SEG, LANES), F32),
        pltpu.VMEM((nrc, nstate, SEG, LANES), F32),
        pltpu.VMEM((nrc, nctx, nstate, LANES), F32),
        pltpu.VMEM((nrc, nctx + 1, nstate, LANES), F32),
        pltpu.VMEM((nrc, nj, SEG, LANES), F32),
        pltpu.VMEM((nrc, seq, LANES), F32),
        pltpu.VMEM((dtokens, width), F32),
        pltpu.VMEM((dtokens, width), F32),
        pltpu.VMEM((dtokens, width), F32),
        pltpu.VMEM((nrc, seq, LANES), F32),
        pltpu.VMEM((dtokens, width), F32),
        pltpu.VMEM((drows, LANES), F32),
        sem((len(args) - 1,)),
    ] + [sem] * 14 + [sem((nreq,))] * 2
    shapes = (jax.ShapeDtypeStruct(inputs.shape, BF16), jax.ShapeDtypeStruct(dec_inputs.shape, BF16))
    return pl.pallas_call(
        functools.partial(kernel, nctx, nch),
        out_shape=tuple(pltpu.VMEM(s.shape, s.dtype) for s in shapes),
        in_specs=[hbm] * 9 + [smem] + [hbm] * 3,
        out_specs=(vmem, vmem),
        scratch_shapes=scratch,
        compiler_params=pltpu.CompilerParams(
            collective_id=0, has_side_effects=True, vmem_limit_bytes=65011712 + 1536 * 1024 - 64 * 1024
        ),
    )(*args)


def solution(mesh):
    placed = (
        P(None, "ctx", "ch"),
        P(None, "ctx", "ch"),
        P(None, "ch"),
        P("ch"),
        P("ch", None),
        P(None, "ch"),
        P("ch"),
        P(None, "ch"),
        P("ch"),
        P(),
        P("ctx"),
        P(None, "ctx", "ch"),
        P(None, "ctx", "ch"),
    )
    return jax.shard_map(
        functools.partial(on_device, mesh.shape["ctx"], mesh.shape["ch"]),
        mesh=mesh,
        in_specs=placed,
        out_specs=(P(None, "ctx", "ch"), P(None, "ctx", "ch")),
        check_vma=False,
    )
```

```python
import functools
import math

import jax
import jax.numpy as jnp
from jax import lax
from jax.experimental import pallas as pl
from jax.experimental.pallas import tpu as pltpu
from jax.sharding import PartitionSpec as P

MESH = pl.DeviceIdType.MESH
F32 = jnp.float32
BF16 = jnp.bfloat16
LOG2E = math.log2(math.e)
KCONV = 4
SEG = 8
LANES = 128
SIDE = 4


def softplus(x):
    return jnp.maximum(x, 0.0) + jnp.log(1.0 + jnp.exp(-jnp.abs(x)))


def silu(x):
    return x / (1.0 + jnp.exp(-x))


def row_of(value, rows=SEG):
    return jnp.broadcast_to(value, (rows, value.shape[1]))


def total_of(terms):
    while len(terms) > 1:
        terms = [a + b for a, b in zip(terms[::2], terms[1::2])] + ([terms[-1]] if len(terms) % 2 else [])
    return terms[0]


def ring(d):
    return min(d, SIDE - d)


def kernel(
    nctx, nch,
    x_hbm, gate_hbm, cw_hbm, cb_hbm, xw_hbm, dtw_hbm, dtb_hbm, a_hbm, skip_hbm, len_ref, req_hbm, dx_hbm, dg_hbm,
    out_ref, dout_ref,
    x_ref, gate_ref, cw_ref, cb_ref, dtw_ref, dtb_ref, a_ref, skip_ref, req_ref, dx_ref, dg_ref,
    hw, xe, u_pre, u_dec, edge_u, edge, send_pre, send_dec, rs_pre, rs_dec, ag_pre, ag_dec, wx, a2, a2b, skips,
    dt_pre, dt_dec, bc_pre, bc_dec, d_all, e_pre, e_dec, ssum, st32, states, hexcl, sexcl, pseg, weight, prefix,
    y_loc, y_nat, y_dec, y_half, g_pre, g_dec, mask_dec,
    in_sems, hw_send, hw_recv, ed_send, ed_recv, rsp_send, rsp_recv, rsd_send, rsd_recv,
    agp_send, agp_recv, agd_send, agd_recv, ss_send, ss_recv, st_send, st_recv,
):
    nreq, seq, width = x_ref.shape
    steps, drows = dx_ref.shape[0], dx_ref.shape[1]
    nstate = a_ref.shape[0]
    rank = dtw_ref.shape[0]
    tokens = nreq * seq
    nj = seq // SEG
    chunks = width // LANES
    nrc = nreq * chunks
    groups = drows // SEG
    part = tokens // nch
    me_ctx = lax.axis_index("ctx")
    me_ch = lax.axis_index("ch")
    offset = me_ctx * seq

    pairs = [
        (x_hbm, x_ref), (xw_hbm, wx.at[pl.ds(0, rank + 2 * nstate)]), (cw_hbm, cw_ref), (cb_hbm, cb_ref), (dx_hbm, dx_ref), (req_hbm, req_ref),
        (dtw_hbm, dtw_ref), (dtb_hbm, dtb_ref), (a_hbm, a_ref), (skip_hbm, skip_ref), (gate_hbm, gate_ref),
        (dg_hbm, dg_ref),
    ]
    loads = []
    for i, (src, dst) in enumerate(pairs):
        sem = in_sems.at[i]
        if len(dst.shape) == 3:
            pieces = [(src.at[k], dst.at[k]) for k in range(dst.shape[0])]
        else:
            pieces = [(src, dst)]
        if i == 0:
            half = pl.ds(0, seq // 2), pl.ds(seq // 2, seq // 2)
            pieces = [(a.at[rows], b.at[rows]) for a, b in pieces for rows in half]
        loads.append((pltpu.make_async_copy(src, dst, sem), [pltpu.make_async_copy(a, b, sem) for a, b in pieces]))

    def begin(some):
        for load, pieces in some:
            for piece in pieces:
                piece.start()

    begin(loads[:2])
    twin = pltpu.make_async_copy(
        xw_hbm.at[pl.ds(rank, 2 * nstate)], wx.at[pl.ds(rank + 2 * nstate, 2 * nstate)], in_sems.at[len(pairs)]
    )
    twin.start()
    begin(loads[2:4])

    def far_ch():
        for k in sorted(range(1, nch), key=lambda k: -(ring(k // SIDE) + ring(k % SIDE))):
            y = lax.rem(me_ch // SIDE + k // SIDE, nch // SIDE)
            z = lax.rem(lax.rem(me_ch, SIDE) + k % SIDE, SIDE)
            yield k, y * SIDE + z

    def far_ctx():
        for k in sorted(range(1, nctx), key=lambda k: -ring(k // 2)):
            x = lax.rem(me_ctx // 2 + k // 2, nctx // 2)
            core = lax.rem(lax.rem(me_ctx, 2) + k % 2, 2)
            yield k, x * 2 + core

    far = {"ch": far_ch, "ctx": far_ctx}

    barrier = pltpu.get_barrier_semaphore()
    for axis in ("ch", "ctx"):
        for k, to in far[axis]():
            pl.semaphore_signal(barrier, inc=1, device_id={axis: to}, device_id_type=MESH)

    begin(loads[4:])

    def spread(axis, src, dst, send_sem, recv_sem):
        for k, to in far[axis]():
            pltpu.make_async_remote_copy(
                src_ref=src(to), dst_ref=dst(k), send_sem=send_sem, recv_sem=recv_sem,
                device_id={axis: to}, device_id_type=MESH,
            ).start()

    def all_of(ref, count, sem):
        view = ref.at[pl.ds(0, count - 1)]
        pltpu.make_async_copy(view, view, sem).wait()

    i0 = lax.broadcasted_iota(jnp.int32, (seq, seq), 0)
    i1 = lax.broadcasted_iota(jnp.int32, (seq, seq), 1)
    perm = jnp.where(i1 == (i0 % SEG) * nj + i0 // SEG, 1.0, 0.0).astype(BF16)
    lane = lax.broadcasted_iota(jnp.int32, (1, LANES), 1)
    low = lane < 2 * nstate
    high = (lane >= 2 * nstate) & (lane < 4 * nstate)

    def split(value):
        top = value.astype(BF16).astype(F32)
        return jnp.where(low, top, jnp.where(high, value - top, 0.0)).astype(BF16)

    def project(u):
        return lax.dot_general(u, wx[...], (((1,), (1,)), ((), ())), preferred_element_type=F32)

    def fill(send, proj):
        send[:, :, pl.ds(0, rank)] = proj[:, :rank].astype(BF16).reshape(nch, part, rank)
        send[:, :, pl.ds(rank, LANES)] = split(proj[:, rank:]).reshape(nch, part, LANES)

    loads[0][0].wait()
    x2 = x_ref[...].reshape(tokens, width)
    q = lax.broadcasted_iota(jnp.int32, (16, tokens), 0)
    col = lax.broadcasted_iota(jnp.int32, (16, tokens), 1)
    win = q >= 6
    q6 = jnp.where(win, q - 6, q)
    second = q6 >= 3
    tap = jnp.where(second, q6 - 3, q6)
    length = jnp.where(second, len_ref[1], len_ref[0])
    target = jnp.where(win, length - (KCONV - 1) + tap - offset, seq - (KCONV - 1) + tap)
    good = (target >= 0) & (target < seq) & (q < 12)
    place = jnp.where(second, seq, 0) + target
    pick = jnp.where(good & (col == place), 1.0, 0.0).astype(BF16)
    hw[me_ctx] = jnp.dot(pick, x2, preferred_element_type=F32).astype(BF16)
    pl.semaphore_wait(barrier, nctx + nch - 2)
    spread("ctx", lambda to: hw.at[me_ctx], lambda k: hw.at[me_ctx], hw_send, hw_recv)

    sub = lax.broadcasted_iota(jnp.int32, (SEG, width), 0)
    for r in range(nreq):
        xe[r, pl.ds(3 * SEG, seq), :] = jnp.dot(perm, x_ref[r], preferred_element_type=F32)
    loads[1][0].wait()
    twin.wait()
    wx[pl.ds(rank + 4 * nstate, LANES - 4 * nstate), :] = jnp.zeros((LANES - 4 * nstate, width), BF16)
    loads[2][0].wait()
    loads[3][0].wait()
    cb = cb_ref[...].reshape(1, width)
    for r in range(nreq):
        for k in range(KCONV - 1):
            last = xe[r, pl.ds((nj + k) * SEG, SEG), :]
            xe[r, pl.ds(k * SEG, SEG), :] = jnp.where(sub == 0, 0.0, pltpu.roll(last, 1, 0))
        conv = cb + sum(cw_ref[k : k + 1] * xe[r, pl.ds(k * SEG, seq), :] for k in range(KCONV))
        u_pre[pl.ds(r * seq, seq), :] = silu(conv).astype(BF16).astype(F32)
    fill(send_pre, project(u_pre[...].astype(BF16)))
    spread("ch", lambda to: send_pre.at[to], lambda k: rs_pre.at[k - 1], rsp_send, rsp_recv)

    for load, _ in loads[4:10]:
        load.wait()
    a2[...] = a_ref[...] * (-LOG2E)
    for c in range(chunks):
        for n in range(nstate):
            a2b[c, n] = row_of(a2[n : n + 1, c * LANES : (c + 1) * LANES])
    dtb = dtb_ref[...].reshape(1, width)
    skip = skip_ref[...].reshape(1, width)
    for c in range(chunks):
        skips[c : c + 1, :] = skip[:, c * LANES : (c + 1) * LANES]
    req = jnp.broadcast_to(req_ref[...].reshape(1, drows), (drows, drows))
    d0 = lax.broadcasted_iota(jnp.int32, (drows, drows), 0)
    d1 = lax.broadcasted_iota(jnp.int32, (drows, drows), 1)
    request = jnp.sum(jnp.where((d0 == d1) & (req == 1), 1.0, 0.0), axis=1, keepdims=True)
    mask_dec[...] = jnp.broadcast_to(request, (drows, LANES))
    edge_u[...] = jnp.zeros_like(edge_u)

    all_of(hw, nctx, hw_recv)
    window = total_of([hw[i].astype(F32) for i in range(nctx)])
    chosen = jnp.broadcast_to(request, (drows, width)) > 0.5
    recent = [
        jnp.where(chosen, row_of(window[9 + k : 10 + k], drows), row_of(window[6 + k : 7 + k], drows))
        for k in range(KCONV - 1)
    ]
    recent = recent + [dx_ref[s].astype(F32) for s in range(steps)]
    for s in range(steps):
        conv = cb + sum(cw_ref[k : k + 1] * recent[s + k] for k in range(KCONV))
        u_dec[pl.ds(s * drows, drows), :] = silu(conv).astype(BF16).astype(F32)
    fill(send_dec, project(u_dec[...].astype(BF16)))
    spread("ch", lambda to: send_dec.at[to], lambda k: rs_dec.at[k - 1], rsd_send, rsd_recv)

    before = hw[lax.rem(me_ctx + nctx - 1, nctx)].astype(F32)
    before = jnp.where(me_ctx > 0, before, 0.0)
    edges = KCONV - 1
    for r in range(nreq):
        for k in range(edges):
            own = xe[r, pl.ds(k * SEG, SEG), :]
            xe[r, pl.ds(k * SEG, SEG), :] = jnp.where(sub == 0, row_of(before[3 * r + k : 3 * r + k + 1]), own)
        conv = cb + sum(cw_ref[k : k + 1] * xe[r, pl.ds(k * SEG, edges * SEG), :] for k in range(KCONV))
        u = silu(conv).astype(BF16).astype(F32)
        u_pre[pl.ds(r * seq, edges * SEG), :] = u
        for k in range(edges):
            edge_u[edges * r + k : edges * r + k + 1, :] = u[k * SEG : k * SEG + 1]
    edge_proj = project(edge_u[...].astype(BF16))
    spot = lax.broadcasted_iota(jnp.int32, (16, LANES), 0)
    left = lax.broadcasted_iota(jnp.int32, (16, LANES), 1)
    count = nreq * edges
    maps = jnp.where(left < 2 * nstate, edge_proj[:, rank:], 0.0)
    packed = jnp.where(spot >= 2 * count, pltpu.roll(maps, 2 * count, 0), 0.0)
    wrapped = pltpu.roll(pltpu.roll(maps, 2 * count - 4, 0), 2 * nstate, 1)
    packed = packed + jnp.where((spot >= 2 * count) & (spot < 3 * count - 4), wrapped, 0.0)
    packed = packed + pltpu.roll(packed, LANES // 2, 1)
    coarse = packed.astype(BF16).astype(F32)
    packed = jnp.where(left < LANES // 2, coarse, packed - coarse)
    lower = pltpu.roll(edge_proj[:, LANES:rank], count, 0)
    packed = jnp.where(spot < count, edge_proj[:, :LANES], jnp.where(spot < 2 * count, lower, packed))
    edge[me_ch] = packed.astype(BF16)
    spread("ch", lambda to: edge.at[me_ch], lambda k: edge.at[me_ch], ed_send, ed_recv)

    def summed(terms):
        total = total_of(terms)
        tail = total[:, rank:]
        tail = tail + pltpu.roll(tail, 2 * nstate, 1) + pltpu.roll(tail, LANES - 2 * nstate, 1)
        return total[:, :rank].astype(BF16), split(tail)

    def reduce(send, rs, ag, rs_recv, ag_send, ag_recv):
        all_of(rs, nch, rs_recv)
        head, tail = summed([send[me_ch].astype(F32)] + [rs[k].astype(F32) for k in range(nch - 1)])
        ag[me_ch, :, pl.ds(0, rank)] = head
        ag[me_ch, :, pl.ds(rank, LANES)] = tail
        spread("ch", lambda to: ag.at[me_ch], lambda k: ag.at[me_ch], ag_send, ag_recv)

    reduce(send_pre, rs_pre, ag_pre, rsp_recv, agp_send, agp_recv)
    for load, _ in loads[10:]:
        load.wait()
    for r in range(nreq):
        for c in range(chunks):
            g_pre[r * chunks + c] = silu(gate_ref[r, :, c * LANES : (c + 1) * LANES].astype(F32))
    for s in range(steps):
        g_dec[pl.ds(s * drows, drows), :] = silu(dg_ref[s].astype(F32))
    reduce(send_dec, rs_dec, ag_dec, rsd_recv, agd_send, agd_recv)

    w0 = lax.broadcasted_iota(jnp.int32, (LANES, 2 * nstate * LANES), 0)
    w1 = lax.broadcasted_iota(jnp.int32, (LANES, 2 * nstate * LANES), 1) // LANES
    copies = jnp.where((w0 == w1) | (w0 == w1 + 2 * nstate), 1.0, 0.0).astype(BF16)

    def expand(proj, bc, ats):
        for at in ats:
            half = pl.ds(at * nstate * LANES, nstate * LANES)
            own = copies[:, at * nstate * LANES : (at + 1) * nstate * LANES]
            bc[:, half] = jnp.dot(proj[:, rank:], own, preferred_element_type=F32)

    def step_sizes(proj):
        return softplus(jnp.dot(proj[:, :rank], dtw_ref[...], preferred_element_type=F32) + dtb)

    all_of(edge, nch, ed_recv)
    whole = total_of([edge[i].astype(F32) for i in range(nch)])
    maps = whole + pltpu.roll(whole, LANES // 2, 1)
    spread_maps = pltpu.roll(maps, 16 - 2 * count, 0)
    wrapped = pltpu.roll(pltpu.roll(maps, 16 - 2 * count + 4, 0), LANES - 2 * nstate, 1)
    maps = jnp.where(spot < 4, spread_maps, wrapped)
    maps = jnp.where(left < 2 * nstate, maps, pltpu.roll(maps, 2 * nstate, 1))
    fixed = jnp.concatenate(
        [
            whole.astype(BF16).astype(F32),
            pltpu.roll(whole, 16 - count, 0).astype(BF16).astype(F32),
            split(maps).astype(F32),
        ],
        axis=1,
    )
    all_of(ag_pre, nch, agp_recv)
    which = lax.broadcasted_iota(jnp.int32, (part, rank + LANES), 0)
    blocks = []
    for p in range(nch):
        block = ag_pre[p]
        spots = [
            (edges * r + k, r * seq + k * SEG - p * part)
            for r in range(nreq)
            for k in range(edges)
            if 0 <= r * seq + k * SEG - p * part < part
        ]
        for at, spot in spots:
            block = jnp.where(which == spot, row_of(fixed[at : at + 1], part), block.astype(F32)).astype(BF16)
        blocks.append(block)
    proj_pre = jnp.concatenate(blocks, axis=0)

    row = lax.broadcasted_iota(jnp.int32, (seq, 1), 0)
    token = offset + (row % SEG) * nj + row // SEG
    sizes = step_sizes(proj_pre)
    for r in range(nreq):
        own = jnp.where(token < len_ref[r], sizes[r * seq : (r + 1) * seq], 0.0)
        dt_pre[pl.ds(r * seq, seq), :] = own
        whole = jnp.sum(own, axis=0, keepdims=True)
        for c in range(chunks):
            ssum[me_ctx, pl.ds(r * chunks + c, 1), :] = whole[:, c * LANES : (c + 1) * LANES]
    spread("ctx", lambda to: ssum.at[me_ctx], lambda k: ssum.at[me_ctx], ss_send, ss_recv)
    expand(proj_pre, bc_pre, (0,))

    sub1 = lax.broadcasted_iota(jnp.int32, (SEG, LANES), 0)

    def lanes_of(c):
        return pl.ds(pl.multiple_of(c * LANES, LANES), LANES)

    def rates(c):
        return [a2b[c, n] for n in range(nstate)]

    def of(n):
        return pl.ds(n * LANES, LANES)

    def first_pass(r):
        def body(c, carry):
            rc = r * chunks + c
            lanes = lanes_of(c)
            rate = rates(c)
            h = [None] * nstate
            total = None
            for j in range(nj):
                rows = pl.ds(r * seq + j * SEG, SEG)
                dt = dt_pre[rows, lanes]
                dtu = dt * u_pre[rows, lanes]
                total = dt if j == 0 else total + dt
                for n in range(nstate):
                    decay = jnp.exp2(dt * rate[n])
                    d_all[rc, j, n] = decay
                    drive = dtu * bc_pre[rows, of(n)]
                    h[n] = drive if j == 0 else decay * h[n] + drive
            for k in (1, 2, 4):
                for n in range(nstate):
                    h[n] = h[n] + jnp.exp2(rate[n] * total) * jnp.where(sub1 >= k, pltpu.roll(h[n], k, 0), 0.0)
                total = total + jnp.where(sub1 >= k, pltpu.roll(total, k, 0), 0.0)
            for n in range(nstate):
                st32[rc, n : n + 1, :] = h[n][SEG - 1 :]
            states[r, me_ctx, c] = st32[rc].astype(BF16)
            sexcl[rc] = jnp.where(sub1 >= 1, pltpu.roll(total, 1, 0), 0.0)
            for n in range(nstate):
                hexcl[rc, n] = jnp.where(sub1 >= 1, pltpu.roll(h[n], 1, 0), 0.0)
            return carry

        for first in range(0, chunks, 2):
            lax.fori_loop(first, first + 2, body, 0)
            own = states.at[r, me_ctx, pl.ds(first, 2)]
            spread("ctx", lambda to: own, lambda k: own, st_send.at[r], st_recv.at[r])

    for r in range(nreq):
        first_pass(r)

    expand(proj_pre, bc_pre, (1,))

    all_of(ag_dec, nch, agd_recv)
    proj_dec = ag_dec[...].reshape(nch * part, rank + LANES)
    dt_dec[...] = step_sizes(proj_dec)
    expand(proj_dec, bc_dec, (0, 1))

    def decode_local(c, carry):
        lanes = lanes_of(c)
        rate = rates(c)
        skipping = row_of(skips[pl.ds(c, 1), :])

        def group(g, carry):
            h, product = [None] * nstate, [None] * nstate
            for s in range(steps):
                rows = pl.ds(pl.multiple_of(s * drows + g * SEG, SEG), SEG)
                dt = dt_dec[rows, lanes]
                u = u_dec[rows, lanes]
                dtu = dt * u
                terms = [skipping * u]
                for n in range(nstate):
                    decay = jnp.exp2(dt * rate[n])
                    cout = bc_dec[rows, of(nstate + n)]
                    drive = dtu * bc_dec[rows, of(n)]
                    h[n] = drive if s == 0 else decay * h[n] + drive
                    product[n] = decay if s == 0 else decay * product[n]
                    terms.append(cout * h[n])
                    e_dec[g * chunks + c, s, n] = cout * product[n]
                y_dec[rows, lanes] = total_of(terms)
            return carry

        return lax.fori_loop(0, groups, group, carry, unroll=8)

    lax.fori_loop(0, chunks, decode_local, 0)

    all_of(ssum, nctx, ss_recv)
    for rc in range(nrc):
        rate = a2[:, (rc % chunks) * LANES : (rc % chunks + 1) * LANES]
        for i in range(nctx):
            weight[rc, i] = jnp.exp2(rate * row_of(ssum[i, rc : rc + 1, :], nstate))

    for r in range(nreq):
        all_of(states.at[r], nctx, st_recv.at[r])
        for c in range(chunks):
            rc = r * chunks + c
            h = jnp.zeros((nstate, LANES), F32)
            for i in range(nctx):
                prefix[rc, i] = h
                h = weight[rc, i] * h + states[r, i, c].astype(F32)
            prefix[rc, nctx] = h

    def prefill_states(rc, carry):
        r, c = rc // chunks, rc % chunks
        lanes = lanes_of(c)
        skipping = row_of(skips[pl.ds(c, 1), :])
        start = sexcl[rc]
        h = [
            hexcl[rc, n]
            + jnp.exp2(a2b[c, n] * start) * row_of(prefix[rc, me_ctx, n : n + 1, :])
            for n in range(nstate)
        ]
        for j in range(nj):
            rows = pl.ds(pl.multiple_of(r * seq + j * SEG, SEG), SEG)
            u = u_pre[rows, lanes]
            dtu = dt_pre[rows, lanes] * u
            terms = [skipping * u]
            for n in range(nstate):
                h[n] = d_all[rc, j, n] * h[n] + dtu * bc_pre[rows, of(n)]
                terms.append(bc_pre[rows, of(nstate + n)] * h[n])
            y_nat[rc, pl.ds(j, SEG, stride=nj), :] = total_of(terms)
        return carry

    lax.fori_loop(0, nrc, prefill_states, 0)

    def decode_rest(c, carry):
        lanes = lanes_of(c)
        half = nstate // 2
        for first in (0, half):
            at = range(first, first + half)
            f0 = [row_of(prefix[c, nctx, n : n + 1, :]) for n in at]
            f1 = [row_of(prefix[chunks + c, nctx, n : n + 1, :]) for n in at]
            for g in range(0, groups, 2):
                pair = []
                for k in (g, g + 1):
                    mine = mask_dec[k * SEG : (k + 1) * SEG, :] > 0.5
                    h = [jnp.where(mine, b, a) for a, b in zip(f0, f1)]
                    done = []
                    for s in range(steps):
                        rows = pl.ds(s * drows + k * SEG, SEG)
                        terms = [e_dec[k * chunks + c, s, n] * h[n - first] for n in at]
                        if first == 0:
                            y_half[rows, lanes] = total_of(terms + [y_dec[rows, lanes]])
                        else:
                            done.append(total_of(terms + [y_half[rows, lanes]]) * g_dec[rows, lanes])
                    pair.append(done)
                for s, (a, b) in enumerate(zip(*pair)):
                    dout_ref[s, pl.ds(g * SEG, 2 * SEG), lanes] = jnp.concatenate([a, b], axis=0).astype(BF16)
        return carry

    lax.fori_loop(0, chunks, decode_rest, 0)

    natural = offset + lax.broadcasted_iota(jnp.int32, (seq, 1), 0)
    for r in range(nreq):
        live = natural < len_ref[r]
        for c in range(chunks):
            y = y_nat[r * chunks + c] * g_pre[r * chunks + c]
            out_ref[r, :, pl.ds(c * LANES, LANES)] = jnp.where(live, y, 0.0).astype(BF16)

    all_of(hw, nctx, hw_send)
    all_of(edge, nch, ed_send)
    all_of(rs_pre, nch, rsp_send)
    all_of(rs_dec, nch, rsd_send)
    all_of(ag_pre, nch, agp_send)
    all_of(ag_dec, nch, agd_send)
    all_of(ssum, nctx, ss_send)
    for r in range(nreq):
        all_of(states.at[r], nctx, st_send.at[r])


def on_device(nctx, nch, *args):
    args = list(args)
    args[4] = args[4].T
    inputs, dt_weight, decay_rate, row_request, dec_inputs = args[0], args[5], args[7], args[10], args[11]
    nreq, seq, width = inputs.shape
    steps, drows = dec_inputs.shape[:2]
    rank, nstate = dt_weight.shape[0], decay_rate.shape[0]
    tokens, dtokens = nreq * seq, steps * drows
    nj, chunks, groups = seq // SEG, width // LANES, drows // SEG
    nrc = nreq * chunks
    cols = rank + LANES
    part, dpart = tokens // nch, dtokens // nch
    hbm = pl.BlockSpec(memory_space=pl.ANY)
    vmem = pl.BlockSpec(memory_space=pltpu.VMEM)
    smem = pl.BlockSpec(memory_space=pltpu.SMEM)
    sem = pltpu.SemaphoreType.DMA
    scratch = [pltpu.VMEM(a.shape, a.dtype) for i, a in enumerate(args) if i not in (4, 9)] + [
        pltpu.VMEM((nctx, 16, width), BF16),
        pltpu.VMEM((nreq, (nj + KCONV - 1) * SEG, width), F32),
        pltpu.VMEM((tokens, width), F32),
        pltpu.VMEM((dtokens, width), F32),
        pltpu.VMEM((16, width), F32),
        pltpu.VMEM((nch, 16, LANES), BF16),
        pltpu.VMEM((nch, part, cols), BF16),
        pltpu.VMEM((nch, dpart, cols), BF16),
        pltpu.VMEM((nch - 1, part, cols), BF16),
        pltpu.VMEM((nch - 1, dpart, cols), BF16),
        pltpu.VMEM((nch, part, cols), BF16),
        pltpu.VMEM((nch, dpart, cols), BF16),
        pltpu.VMEM((cols, width), BF16),
        pltpu.VMEM((nstate, width), F32),
        pltpu.VMEM((chunks, nstate, SEG, LANES), F32),
        pltpu.VMEM((8, LANES), F32),
        pltpu.VMEM((tokens, width), F32),
        pltpu.VMEM((dtokens, width), F32),
        pltpu.VMEM((tokens, 2 * nstate * LANES), F32),
        pltpu.VMEM((dtokens, 2 * nstate * LANES), F32),
        pltpu.VMEM((nrc, nj, nstate, SEG, LANES), F32),
        pltpu.VMEM((nrc, nj, nstate, SEG, LANES), F32),
        pltpu.VMEM((groups * chunks, steps, nstate, SEG, LANES), F32),
        pltpu.VMEM((nctx, nrc, LANES), F32),
        pltpu.VMEM((nrc, nstate, LANES), F32),
        pltpu.VMEM((nreq, nctx, chunks, nstate, LANES), BF16),
        pltpu.VMEM((nrc, nstate, SEG, LANES), F32),
        pltpu.VMEM((nrc, SEG, LANES), F32),
        pltpu.VMEM((nrc, nstate, SEG, LANES), F32),
        pltpu.VMEM((nrc, nctx, nstate, LANES), F32),
        pltpu.VMEM((nrc, nctx + 1, nstate, LANES), F32),
        pltpu.VMEM((nrc, nj, SEG, LANES), F32),
        pltpu.VMEM((nrc, seq, LANES), F32),
        pltpu.VMEM((dtokens, width), F32),
        pltpu.VMEM((dtokens, width), F32),
        pltpu.VMEM((nrc, seq, LANES), F32),
        pltpu.VMEM((dtokens, width), F32),
        pltpu.VMEM((drows, LANES), F32),
        sem((len(args),)),
    ] + [sem] * 14 + [sem((nreq,))] * 2
    shapes = (jax.ShapeDtypeStruct(inputs.shape, BF16), jax.ShapeDtypeStruct(dec_inputs.shape, BF16))
    return pl.pallas_call(
        functools.partial(kernel, nctx, nch),
        out_shape=tuple(pltpu.VMEM(s.shape, s.dtype) for s in shapes),
        in_specs=[hbm] * 9 + [smem] + [hbm] * 3,
        out_specs=(vmem, vmem),
        scratch_shapes=scratch,
        compiler_params=pltpu.CompilerParams(
            collective_id=0, has_side_effects=True, vmem_limit_bytes=65011712 + 1536 * 1024 - 64 * 1024
        ),
    )(*args)


def solution(mesh):
    placed = (
        P(None, "ctx", "ch"),
        P(None, "ctx", "ch"),
        P(None, "ch"),
        P("ch"),
        P("ch", None),
        P(None, "ch"),
        P("ch"),
        P(None, "ch"),
        P("ch"),
        P(),
        P("ctx"),
        P(None, "ctx", "ch"),
        P(None, "ctx", "ch"),
    )
    return jax.shard_map(
        functools.partial(on_device, mesh.shape["ctx"], mesh.shape["ch"]),
        mesh=mesh,
        in_specs=placed,
        out_specs=(P(None, "ctx", "ch"), P(None, "ctx", "ch")),
        check_vma=False,
    )
```

```python
import functools
import math

import jax
import jax.numpy as jnp
from jax import lax
from jax.experimental import pallas as pl
from jax.experimental.pallas import tpu as pltpu
from jax.sharding import PartitionSpec as P

MESH = pl.DeviceIdType.MESH
F32 = jnp.float32
BF16 = jnp.bfloat16
LOG2E = math.log2(math.e)
KCONV = 4
SEG = 8
LANES = 128
SIDE = 4


def softplus(x):
    return jnp.maximum(x, 0.0) + jnp.log(1.0 + jnp.exp(-jnp.abs(x)))


def silu(x):
    return x / (1.0 + jnp.exp(-x))


def row_of(value, rows=SEG):
    return jnp.broadcast_to(value, (rows, value.shape[1]))


def total_of(terms):
    while len(terms) > 1:
        terms = [a + b for a, b in zip(terms[::2], terms[1::2])] + ([terms[-1]] if len(terms) % 2 else [])
    return terms[0]


def ring(d):
    return min(d, SIDE - d)


def kernel(
    nctx, nch,
    x_hbm, gate_hbm, cw_hbm, cb_hbm, xw_hbm, dtw_hbm, dtb_hbm, a_hbm, skip_hbm, len_ref, req_hbm, dx_hbm, dg_hbm,
    out_ref, dout_ref,
    x_ref, gate_ref, cw_ref, cb_ref, dtw_ref, dtb_ref, a_ref, skip_ref, req_ref, dx_ref, dg_ref,
    hw, xe, u_pre, u_dec, edge_u, edge, send_pre, send_dec, rs_pre, rs_dec, ag_pre, ag_dec, wx, a2, a2b, skips,
    dt_pre, dt_dec, bc_pre, bc_dec, d_all, e_pre, e_dec, ssum, st32, states, hexcl, sexcl, pseg, weight, prefix,
    y_loc, y_nat, y_dec, y_half, g_pre, g_dec, mask_dec,
    in_sems, hw_send, hw_recv, ed_send, ed_recv, rsp_send, rsp_recv, rsd_send, rsd_recv,
    agp_send, agp_recv, agd_send, agd_recv, ss_send, ss_recv, st_send, st_recv,
):
    nreq, seq, width = x_ref.shape
    steps, drows = dx_ref.shape[0], dx_ref.shape[1]
    nstate = a_ref.shape[0]
    rank = dtw_ref.shape[0]
    tokens = nreq * seq
    nj = seq // SEG
    chunks = width // LANES
    nrc = nreq * chunks
    groups = drows // SEG
    part = tokens // nch
    me_ctx = lax.axis_index("ctx")
    me_ch = lax.axis_index("ch")
    offset = me_ctx * seq

    pairs = [
        (x_hbm, x_ref), (xw_hbm, wx.at[pl.ds(0, rank + 2 * nstate)]), (cw_hbm, cw_ref), (cb_hbm, cb_ref), (dx_hbm, dx_ref), (req_hbm, req_ref),
        (dtw_hbm, dtw_ref), (dtb_hbm, dtb_ref), (a_hbm, a_ref), (skip_hbm, skip_ref), (gate_hbm, gate_ref),
        (dg_hbm, dg_ref),
    ]
    loads = []
    for i, (src, dst) in enumerate(pairs):
        sem = in_sems.at[i]
        if len(dst.shape) == 3:
            pieces = [(src.at[k], dst.at[k]) for k in range(dst.shape[0])]
        else:
            pieces = [(src, dst)]
        if i == 0:
            half = pl.ds(0, seq // 2), pl.ds(seq // 2, seq // 2)
            pieces = [(a.at[rows], b.at[rows]) for a, b in pieces for rows in half]
        loads.append((pltpu.make_async_copy(src, dst, sem), [pltpu.make_async_copy(a, b, sem) for a, b in pieces]))

    def begin(some):
        for load, pieces in some:
            for piece in pieces:
                piece.start()

    begin(loads[:2])
    twin = pltpu.make_async_copy(
        xw_hbm.at[pl.ds(rank, 2 * nstate)], wx.at[pl.ds(rank + 2 * nstate, 2 * nstate)], in_sems.at[len(pairs)]
    )
    twin.start()
    begin(loads[2:4])

    def far_ch():
        for k in sorted(range(1, nch), key=lambda k: -(ring(k // SIDE) + ring(k % SIDE))):
            y = lax.rem(me_ch // SIDE + k // SIDE, nch // SIDE)
            z = lax.rem(lax.rem(me_ch, SIDE) + k % SIDE, SIDE)
            yield k, y * SIDE + z

    def far_ctx():
        for k in sorted(range(1, nctx), key=lambda k: -ring(k // 2)):
            x = lax.rem(me_ctx // 2 + k // 2, nctx // 2)
            core = lax.rem(lax.rem(me_ctx, 2) + k % 2, 2)
            yield k, x * 2 + core

    far = {"ch": far_ch, "ctx": far_ctx}

    barrier = pltpu.get_barrier_semaphore()
    for axis in ("ch", "ctx"):
        for k, to in far[axis]():
            pl.semaphore_signal(barrier, inc=1, device_id={axis: to}, device_id_type=MESH)

    begin(loads[4:])

    def spread(axis, src, dst, send_sem, recv_sem):
        for k, to in far[axis]():
            pltpu.make_async_remote_copy(
                src_ref=src(to), dst_ref=dst(k), send_sem=send_sem, recv_sem=recv_sem,
                device_id={axis: to}, device_id_type=MESH,
            ).start()

    def all_of(ref, count, sem):
        view = ref.at[pl.ds(0, count - 1)]
        pltpu.make_async_copy(view, view, sem).wait()

    i0 = lax.broadcasted_iota(jnp.int32, (seq, seq), 0)
    i1 = lax.broadcasted_iota(jnp.int32, (seq, seq), 1)
    perm = jnp.where(i1 == (i0 % SEG) * nj + i0 // SEG, 1.0, 0.0).astype(BF16)
    lane = lax.broadcasted_iota(jnp.int32, (1, LANES), 1)
    low = lane < 2 * nstate
    high = (lane >= 2 * nstate) & (lane < 4 * nstate)

    def split(value):
        top = value.astype(BF16).astype(F32)
        return jnp.where(low, top, jnp.where(high, value - top, 0.0)).astype(BF16)

    def project(u):
        return lax.dot_general(u, wx[...], (((1,), (1,)), ((), ())), preferred_element_type=F32)

    def fill(send, proj):
        send[:, :, pl.ds(0, rank)] = proj[:, :rank].astype(BF16).reshape(nch, part, rank)
        send[:, :, pl.ds(rank, LANES)] = split(proj[:, rank:]).reshape(nch, part, LANES)

    loads[0][0].wait()
    x2 = x_ref[...].reshape(tokens, width)
    q = lax.broadcasted_iota(jnp.int32, (16, tokens), 0)
    col = lax.broadcasted_iota(jnp.int32, (16, tokens), 1)
    win = q >= 6
    q6 = jnp.where(win, q - 6, q)
    second = q6 >= 3
    tap = jnp.where(second, q6 - 3, q6)
    length = jnp.where(second, len_ref[1], len_ref[0])
    target = jnp.where(win, length - (KCONV - 1) + tap - offset, seq - (KCONV - 1) + tap)
    good = (target >= 0) & (target < seq) & (q < 12)
    place = jnp.where(second, seq, 0) + target
    pick = jnp.where(good & (col == place), 1.0, 0.0).astype(BF16)
    hw[me_ctx] = jnp.dot(pick, x2, preferred_element_type=F32).astype(BF16)
    pl.semaphore_wait(barrier, nctx + nch - 2)
    spread("ctx", lambda to: hw.at[me_ctx], lambda k: hw.at[me_ctx], hw_send, hw_recv)

    sub = lax.broadcasted_iota(jnp.int32, (SEG, width), 0)
    for r in range(nreq):
        xe[r, pl.ds(3 * SEG, seq), :] = jnp.dot(perm, x_ref[r], preferred_element_type=F32)
    loads[1][0].wait()
    twin.wait()
    wx[pl.ds(rank + 4 * nstate, LANES - 4 * nstate), :] = jnp.zeros((LANES - 4 * nstate, width), BF16)
    loads[2][0].wait()
    loads[3][0].wait()
    cb = cb_ref[...].reshape(1, width)
    for r in range(nreq):
        for k in range(KCONV - 1):
            last = xe[r, pl.ds((nj + k) * SEG, SEG), :]
            xe[r, pl.ds(k * SEG, SEG), :] = jnp.where(sub == 0, 0.0, pltpu.roll(last, 1, 0))
        conv = cb + sum(cw_ref[k : k + 1] * xe[r, pl.ds(k * SEG, seq), :] for k in range(KCONV))
        u_pre[pl.ds(r * seq, seq), :] = silu(conv).astype(BF16).astype(F32)
    fill(send_pre, project(u_pre[...].astype(BF16)))
    spread("ch", lambda to: send_pre.at[to], lambda k: rs_pre.at[k - 1], rsp_send, rsp_recv)

    for load, _ in loads[4:10]:
        load.wait()
    a2[...] = a_ref[...] * (-LOG2E)
    for c in range(chunks):
        for n in range(nstate):
            a2b[c, n] = row_of(a2[n : n + 1, c * LANES : (c + 1) * LANES])
    dtb = dtb_ref[...].reshape(1, width)
    skip = skip_ref[...].reshape(1, width)
    for c in range(chunks):
        skips[c : c + 1, :] = skip[:, c * LANES : (c + 1) * LANES]
    req = jnp.broadcast_to(req_ref[...].reshape(1, drows), (drows, drows))
    d0 = lax.broadcasted_iota(jnp.int32, (drows, drows), 0)
    d1 = lax.broadcasted_iota(jnp.int32, (drows, drows), 1)
    request = jnp.sum(jnp.where((d0 == d1) & (req == 1), 1.0, 0.0), axis=1, keepdims=True)
    mask_dec[...] = jnp.broadcast_to(request, (drows, LANES))
    edge_u[...] = jnp.zeros_like(edge_u)

    for s in range(steps):
        rows = pl.ds(s * drows, drows)
        known = cb + sum(
            cw_ref[k : k + 1] * dx_ref[s + k - KCONV + 1].astype(F32) for k in range(max(KCONV - 1 - s, 0), KCONV)
        )
        if s < KCONV - 1:
            y_dec[rows, :] = known
        else:
            u_dec[rows, :] = silu(known).astype(BF16).astype(F32)
    all_of(hw, nctx, hw_recv)
    window = total_of([hw[i].astype(F32) for i in range(nctx)])
    chosen = jnp.broadcast_to(request, (drows, width)) > 0.5
    recent = [
        jnp.where(chosen, row_of(window[9 + k : 10 + k], drows), row_of(window[6 + k : 7 + k], drows))
        for k in range(KCONV - 1)
    ]
    for s in range(KCONV - 1):
        rows = pl.ds(s * drows, drows)
        conv = y_dec[rows, :] + sum(cw_ref[k : k + 1] * recent[s + k] for k in range(KCONV - 1 - s))
        u_dec[rows, :] = silu(conv).astype(BF16).astype(F32)
    fill(send_dec, project(u_dec[...].astype(BF16)))
    spread("ch", lambda to: send_dec.at[to], lambda k: rs_dec.at[k - 1], rsd_send, rsd_recv)

    before = hw[lax.rem(me_ctx + nctx - 1, nctx)].astype(F32)
    before = jnp.where(me_ctx > 0, before, 0.0)
    edges = KCONV - 1
    for r in range(nreq):
        for k in range(edges):
            own = xe[r, pl.ds(k * SEG, SEG), :]
            xe[r, pl.ds(k * SEG, SEG), :] = jnp.where(sub == 0, row_of(before[3 * r + k : 3 * r + k + 1]), own)
        conv = cb + sum(cw_ref[k : k + 1] * xe[r, pl.ds(k * SEG, edges * SEG), :] for k in range(KCONV))
        u = silu(conv).astype(BF16).astype(F32)
        u_pre[pl.ds(r * seq, edges * SEG), :] = u
        for k in range(edges):
            edge_u[edges * r + k : edges * r + k + 1, :] = u[k * SEG : k * SEG + 1]
    edge_proj = project(edge_u[...].astype(BF16))
    spot = lax.broadcasted_iota(jnp.int32, (16, LANES), 0)
    left = lax.broadcasted_iota(jnp.int32, (16, LANES), 1)
    count = nreq * edges
    maps = jnp.where(left < 2 * nstate, edge_proj[:, rank:], 0.0)
    packed = jnp.where(spot >= 2 * count, pltpu.roll(maps, 2 * count, 0), 0.0)
    wrapped = pltpu.roll(pltpu.roll(maps, 2 * count - 4, 0), 2 * nstate, 1)
    packed = packed + jnp.where((spot >= 2 * count) & (spot < 3 * count - 4), wrapped, 0.0)
    packed = packed + pltpu.roll(packed, LANES // 2, 1)
    coarse = packed.astype(BF16).astype(F32)
    packed = jnp.where(left < LANES // 2, coarse, packed - coarse)
    lower = pltpu.roll(edge_proj[:, LANES:rank], count, 0)
    packed = jnp.where(spot < count, edge_proj[:, :LANES], jnp.where(spot < 2 * count, lower, packed))
    edge[me_ch] = packed.astype(BF16)
    spread("ch", lambda to: edge.at[me_ch], lambda k: edge.at[me_ch], ed_send, ed_recv)

    def summed(terms):
        total = total_of(terms)
        tail = total[:, rank:]
        tail = tail + pltpu.roll(tail, 2 * nstate, 1) + pltpu.roll(tail, LANES - 2 * nstate, 1)
        return total[:, :rank].astype(BF16), split(tail)

    def reduce(send, rs, ag, rs_recv, ag_send, ag_recv):
        all_of(rs, nch, rs_recv)
        head, tail = summed([send[me_ch].astype(F32)] + [rs[k].astype(F32) for k in range(nch - 1)])
        ag[me_ch, :, pl.ds(0, rank)] = head
        ag[me_ch, :, pl.ds(rank, LANES)] = tail
        spread("ch", lambda to: ag.at[me_ch], lambda k: ag.at[me_ch], ag_send, ag_recv)

    reduce(send_pre, rs_pre, ag_pre, rsp_recv, agp_send, agp_recv)
    for load, _ in loads[10:]:
        load.wait()
    for r in range(nreq):
        for c in range(chunks):
            g_pre[r * chunks + c] = silu(gate_ref[r, :, c * LANES : (c + 1) * LANES].astype(F32))
    for s in range(steps):
        g_dec[pl.ds(s * drows, drows), :] = silu(dg_ref[s].astype(F32))
    reduce(send_dec, rs_dec, ag_dec, rsd_recv, agd_send, agd_recv)

    w0 = lax.broadcasted_iota(jnp.int32, (LANES, 2 * nstate * LANES), 0)
    w1 = lax.broadcasted_iota(jnp.int32, (LANES, 2 * nstate * LANES), 1) // LANES
    copies = jnp.where((w0 == w1) | (w0 == w1 + 2 * nstate), 1.0, 0.0).astype(BF16)

    def expand(proj, bc, ats):
        for at in ats:
            half = pl.ds(at * nstate * LANES, nstate * LANES)
            own = copies[:, at * nstate * LANES : (at + 1) * nstate * LANES]
            bc[:, half] = jnp.dot(proj[:, rank:], own, preferred_element_type=F32)

    def step_sizes(proj):
        return softplus(jnp.dot(proj[:, :rank], dtw_ref[...], preferred_element_type=F32) + dtb)

    all_of(edge, nch, ed_recv)
    whole = total_of([edge[i].astype(F32) for i in range(nch)])
    maps = whole + pltpu.roll(whole, LANES // 2, 1)
    spread_maps = pltpu.roll(maps, 16 - 2 * count, 0)
    wrapped = pltpu.roll(pltpu.roll(maps, 16 - 2 * count + 4, 0), LANES - 2 * nstate, 1)
    maps = jnp.where(spot < 4, spread_maps, wrapped)
    maps = jnp.where(left < 2 * nstate, maps, pltpu.roll(maps, 2 * nstate, 1))
    fixed = jnp.concatenate(
        [
            whole.astype(BF16).astype(F32),
            pltpu.roll(whole, 16 - count, 0).astype(BF16).astype(F32),
            split(maps).astype(F32),
        ],
        axis=1,
    )
    all_of(ag_pre, nch, agp_recv)
    which = lax.broadcasted_iota(jnp.int32, (part, rank + LANES), 0)
    blocks = []
    for p in range(nch):
        block = ag_pre[p]
        spots = [
            (edges * r + k, r * seq + k * SEG - p * part)
            for r in range(nreq)
            for k in range(edges)
            if 0 <= r * seq + k * SEG - p * part < part
        ]
        for at, spot in spots:
            block = jnp.where(which == spot, row_of(fixed[at : at + 1], part), block.astype(F32)).astype(BF16)
        blocks.append(block)
    proj_pre = jnp.concatenate(blocks, axis=0)

    row = lax.broadcasted_iota(jnp.int32, (seq, 1), 0)
    token = offset + (row % SEG) * nj + row // SEG
    sizes = step_sizes(proj_pre)
    for r in range(nreq):
        own = jnp.where(token < len_ref[r], sizes[r * seq : (r + 1) * seq], 0.0)
        dt_pre[pl.ds(r * seq, seq), :] = own
        whole = jnp.sum(own, axis=0, keepdims=True)
        for c in range(chunks):
            ssum[me_ctx, pl.ds(r * chunks + c, 1), :] = whole[:, c * LANES : (c + 1) * LANES]
    spread("ctx", lambda to: ssum.at[me_ctx], lambda k: ssum.at[me_ctx], ss_send, ss_recv)
    expand(proj_pre, bc_pre, (0,))

    sub1 = lax.broadcasted_iota(jnp.int32, (SEG, LANES), 0)

    def lanes_of(c):
        return pl.ds(pl.multiple_of(c * LANES, LANES), LANES)

    def rates(c):
        return [a2b[c, n] for n in range(nstate)]

    def of(n):
        return pl.ds(n * LANES, LANES)

    def first_pass(r):
        def body(c, carry):
            rc = r * chunks + c
            lanes = lanes_of(c)
            rate = rates(c)
            h = [None] * nstate
            total = None
            for j in range(nj):
                rows = pl.ds(r * seq + j * SEG, SEG)
                dt = dt_pre[rows, lanes]
                dtu = dt * u_pre[rows, lanes]
                total = dt if j == 0 else total + dt
                for n in range(nstate):
                    decay = jnp.exp2(dt * rate[n])
                    d_all[rc, j, n] = decay
                    drive = dtu * bc_pre[rows, of(n)]
                    h[n] = drive if j == 0 else decay * h[n] + drive
            for k in (1, 2, 4):
                for n in range(nstate):
                    h[n] = h[n] + jnp.exp2(rate[n] * total) * jnp.where(sub1 >= k, pltpu.roll(h[n], k, 0), 0.0)
                total = total + jnp.where(sub1 >= k, pltpu.roll(total, k, 0), 0.0)
            for n in range(nstate):
                st32[rc, n : n + 1, :] = h[n][SEG - 1 :]
            states[r, me_ctx, c] = st32[rc].astype(BF16)
            sexcl[rc] = jnp.where(sub1 >= 1, pltpu.roll(total, 1, 0), 0.0)
            for n in range(nstate):
                hexcl[rc, n] = jnp.where(sub1 >= 1, pltpu.roll(h[n], 1, 0), 0.0)
            return carry

        for first in range(0, chunks, 2):
            lax.fori_loop(first, first + 2, body, 0)
            own = states.at[r, me_ctx, pl.ds(first, 2)]
            spread("ctx", lambda to: own, lambda k: own, st_send.at[r], st_recv.at[r])

    for r in range(nreq):
        first_pass(r)

    expand(proj_pre, bc_pre, (1,))

    all_of(ag_dec, nch, agd_recv)
    proj_dec = ag_dec[...].reshape(nch * part, rank + LANES)
    dt_dec[...] = step_sizes(proj_dec)
    expand(proj_dec, bc_dec, (0, 1))

    def decode_local(c, carry):
        lanes = lanes_of(c)
        rate = rates(c)
        skipping = row_of(skips[pl.ds(c, 1), :])

        def group(g, carry):
            h, product = [None] * nstate, [None] * nstate
            for s in range(steps):
                rows = pl.ds(pl.multiple_of(s * drows + g * SEG, SEG), SEG)
                dt = dt_dec[rows, lanes]
                u = u_dec[rows, lanes]
                dtu = dt * u
                terms = [skipping * u]
                for n in range(nstate):
                    decay = jnp.exp2(dt * rate[n])
                    cout = bc_dec[rows, of(nstate + n)]
                    drive = dtu * bc_dec[rows, of(n)]
                    h[n] = drive if s == 0 else decay * h[n] + drive
                    product[n] = decay if s == 0 else decay * product[n]
                    terms.append(cout * h[n])
                    e_dec[g * chunks + c, s, n] = cout * product[n]
                y_dec[rows, lanes] = total_of(terms)
            return carry

        return lax.fori_loop(0, groups, group, carry, unroll=8)

    lax.fori_loop(0, chunks, decode_local, 0)

    all_of(ssum, nctx, ss_recv)
    for rc in range(nrc):
        rate = a2[:, (rc % chunks) * LANES : (rc % chunks + 1) * LANES]
        for i in range(nctx):
            weight[rc, i] = jnp.exp2(rate * row_of(ssum[i, rc : rc + 1, :], nstate))

    for r in range(nreq):
        all_of(states.at[r], nctx, st_recv.at[r])
        for c in range(chunks):
            rc = r * chunks + c
            h = jnp.zeros((nstate, LANES), F32)
            for i in range(nctx):
                prefix[rc, i] = h
                h = weight[rc, i] * h + states[r, i, c].astype(F32)
            prefix[rc, nctx] = h

    def prefill_states(rc, carry):
        r, c = rc // chunks, rc % chunks
        lanes = lanes_of(c)
        skipping = row_of(skips[pl.ds(c, 1), :])
        start = sexcl[rc]
        h = [
            hexcl[rc, n]
            + jnp.exp2(a2b[c, n] * start) * row_of(prefix[rc, me_ctx, n : n + 1, :])
            for n in range(nstate)
        ]
        for j in range(nj):
            rows = pl.ds(pl.multiple_of(r * seq + j * SEG, SEG), SEG)
            u = u_pre[rows, lanes]
            dtu = dt_pre[rows, lanes] * u
            terms = [skipping * u]
            for n in range(nstate):
                h[n] = d_all[rc, j, n] * h[n] + dtu * bc_pre[rows, of(n)]
                terms.append(bc_pre[rows, of(nstate + n)] * h[n])
            y_nat[rc, pl.ds(j, SEG, stride=nj), :] = total_of(terms)
        return carry

    lax.fori_loop(0, nrc, prefill_states, 0)

    def decode_rest(c, carry):
        lanes = lanes_of(c)
        half = nstate // 2
        for first in (0, half):
            at = range(first, first + half)
            f0 = [row_of(prefix[c, nctx, n : n + 1, :]) for n in at]
            f1 = [row_of(prefix[chunks + c, nctx, n : n + 1, :]) for n in at]
            for g in range(0, groups, 2):
                pair = []
                for k in (g, g + 1):
                    mine = mask_dec[k * SEG : (k + 1) * SEG, :] > 0.5
                    h = [jnp.where(mine, b, a) for a, b in zip(f0, f1)]
                    done = []
                    for s in range(steps):
                        rows = pl.ds(s * drows + k * SEG, SEG)
                        terms = [e_dec[k * chunks + c, s, n] * h[n - first] for n in at]
                        if first == 0:
                            y_half[rows, lanes] = total_of(terms + [y_dec[rows, lanes]])
                        else:
                            done.append(total_of(terms + [y_half[rows, lanes]]) * g_dec[rows, lanes])
                    pair.append(done)
                for s, (a, b) in enumerate(zip(*pair)):
                    dout_ref[s, pl.ds(g * SEG, 2 * SEG), lanes] = jnp.concatenate([a, b], axis=0).astype(BF16)
        return carry

    lax.fori_loop(0, chunks, decode_rest, 0)

    natural = offset + lax.broadcasted_iota(jnp.int32, (seq, 1), 0)
    for r in range(nreq):
        live = natural < len_ref[r]
        for c in range(chunks):
            y = y_nat[r * chunks + c] * g_pre[r * chunks + c]
            out_ref[r, :, pl.ds(c * LANES, LANES)] = jnp.where(live, y, 0.0).astype(BF16)

    all_of(hw, nctx, hw_send)
    all_of(edge, nch, ed_send)
    all_of(rs_pre, nch, rsp_send)
    all_of(rs_dec, nch, rsd_send)
    all_of(ag_pre, nch, agp_send)
    all_of(ag_dec, nch, agd_send)
    all_of(ssum, nctx, ss_send)
    for r in range(nreq):
        all_of(states.at[r], nctx, st_send.at[r])


def on_device(nctx, nch, *args):
    args = list(args)
    args[4] = args[4].T
    inputs, dt_weight, decay_rate, row_request, dec_inputs = args[0], args[5], args[7], args[10], args[11]
    nreq, seq, width = inputs.shape
    steps, drows = dec_inputs.shape[:2]
    rank, nstate = dt_weight.shape[0], decay_rate.shape[0]
    tokens, dtokens = nreq * seq, steps * drows
    nj, chunks, groups = seq // SEG, width // LANES, drows // SEG
    nrc = nreq * chunks
    cols = rank + LANES
    part, dpart = tokens // nch, dtokens // nch
    hbm = pl.BlockSpec(memory_space=pl.ANY)
    vmem = pl.BlockSpec(memory_space=pltpu.VMEM)
    smem = pl.BlockSpec(memory_space=pltpu.SMEM)
    sem = pltpu.SemaphoreType.DMA
    scratch = [pltpu.VMEM(a.shape, a.dtype) for i, a in enumerate(args) if i not in (4, 9)] + [
        pltpu.VMEM((nctx, 16, width), BF16),
        pltpu.VMEM((nreq, (nj + KCONV - 1) * SEG, width), F32),
        pltpu.VMEM((tokens, width), F32),
        pltpu.VMEM((dtokens, width), F32),
        pltpu.VMEM((16, width), F32),
        pltpu.VMEM((nch, 16, LANES), BF16),
        pltpu.VMEM((nch, part, cols), BF16),
        pltpu.VMEM((nch, dpart, cols), BF16),
        pltpu.VMEM((nch - 1, part, cols), BF16),
        pltpu.VMEM((nch - 1, dpart, cols), BF16),
        pltpu.VMEM((nch, part, cols), BF16),
        pltpu.VMEM((nch, dpart, cols), BF16),
        pltpu.VMEM((cols, width), BF16),
        pltpu.VMEM((nstate, width), F32),
        pltpu.VMEM((chunks, nstate, SEG, LANES), F32),
        pltpu.VMEM((8, LANES), F32),
        pltpu.VMEM((tokens, width), F32),
        pltpu.VMEM((dtokens, width), F32),
        pltpu.VMEM((tokens, 2 * nstate * LANES), F32),
        pltpu.VMEM((dtokens, 2 * nstate * LANES), F32),
        pltpu.VMEM((nrc, nj, nstate, SEG, LANES), F32),
        pltpu.VMEM((nrc, nj, nstate, SEG, LANES), F32),
        pltpu.VMEM((groups * chunks, steps, nstate, SEG, LANES), F32),
        pltpu.VMEM((nctx, nrc, LANES), F32),
        pltpu.VMEM((nrc, nstate, LANES), F32),
        pltpu.VMEM((nreq, nctx, chunks, nstate, LANES), BF16),
        pltpu.VMEM((nrc, nstate, SEG, LANES), F32),
        pltpu.VMEM((nrc, SEG, LANES), F32),
        pltpu.VMEM((nrc, nstate, SEG, LANES), F32),
        pltpu.VMEM((nrc, nctx, nstate, LANES), F32),
        pltpu.VMEM((nrc, nctx + 1, nstate, LANES), F32),
        pltpu.VMEM((nrc, nj, SEG, LANES), F32),
        pltpu.VMEM((nrc, seq, LANES), F32),
        pltpu.VMEM((dtokens, width), F32),
        pltpu.VMEM((dtokens, width), F32),
        pltpu.VMEM((nrc, seq, LANES), F32),
        pltpu.VMEM((dtokens, width), F32),
        pltpu.VMEM((drows, LANES), F32),
        sem((len(args),)),
    ] + [sem] * 14 + [sem((nreq,))] * 2
    shapes = (jax.ShapeDtypeStruct(inputs.shape, BF16), jax.ShapeDtypeStruct(dec_inputs.shape, BF16))
    return pl.pallas_call(
        functools.partial(kernel, nctx, nch),
        out_shape=tuple(pltpu.VMEM(s.shape, s.dtype) for s in shapes),
        in_specs=[hbm] * 9 + [smem] + [hbm] * 3,
        out_specs=(vmem, vmem),
        scratch_shapes=scratch,
        compiler_params=pltpu.CompilerParams(
            collective_id=0, has_side_effects=True, vmem_limit_bytes=65011712 + 1536 * 1024 - 64 * 1024
        ),
    )(*args)


def solution(mesh):
    placed = (
        P(None, "ctx", "ch"),
        P(None, "ctx", "ch"),
        P(None, "ch"),
        P("ch"),
        P("ch", None),
        P(None, "ch"),
        P("ch"),
        P(None, "ch"),
        P("ch"),
        P(),
        P("ctx"),
        P(None, "ctx", "ch"),
        P(None, "ctx", "ch"),
    )
    return jax.shard_map(
        functools.partial(on_device, mesh.shape["ctx"], mesh.shape["ch"]),
        mesh=mesh,
        in_specs=placed,
        out_specs=(P(None, "ctx", "ch"), P(None, "ctx", "ch")),
        check_vma=False,
    )
```
